256 devices in a mesh: wide: 32 (over z, x), tensor: 8 (over y, core).
Axes of the slice: x: 4, y: 4, z: 8, core: 2. Of those that a mesh axis runs over, the one named last changes fastest.
Arguments:
- queries: bfloat16 [4, 2048, 8192], P(None, 'wide', 'tensor'), may hold values from -6 to 6
- new_keys: bfloat16 [4, 2048, 1024], P(None, 'wide', 'tensor'), may hold values from -4.5 to 4.5
- new_values: bfloat16 [4, 2048, 1024], P(None, 'wide', 'tensor'), may hold values from -4.5 to 4.5
- suffix_keys: bfloat16 [2048, 64, 1024], P('wide', None, 'tensor'), may hold values from -4.5 to 4.5
- suffix_values: bfloat16 [2048, 64, 1024], P('wide', None, 'tensor'), may hold values from -4.5 to 4.5
- suffix_len: int32 [2048], P('wide'), may hold values from 1 to 64, 65536 in all
- prefix_keys: bfloat16 [64, 768, 1024], P('wide', None, 'tensor'), may hold values from -4.5 to 4.5
- prefix_values: bfloat16 [64, 768, 1024], P('wide', None, 'tensor'), may hold values from -4.5 to 4.5
- prefix_of: int32 [2048, 1], P('wide'), may hold values from 0 to 63; in each aligned block of 64 rows (0 to 63, 64 to 127, ...) at most 2 rows name the same one
- out_weight: bfloat16 [8192, 4096], P('tensor'), may hold values from -0.09375 to 0.09375
Outputs:
- projected: bfloat16 [4, 2048, 4096], P(None, 'wide', 'tensor')
The draws below stay inside these ranges and needn't reach their ends.
Inputs may be any that keep to these rules, and one draw needn't show every extreme that they name: `prefix_of`: among the 64 requests of one index of wide, no prompt is named more than 2 times, and in some such block one prompt is named exactly 2 times; every prompt is named by some request. `suffix_len`: some request has exactly 64 valid rows.
All inputs are finite; a program needn't handle non-finite values. No bound on the sum of `suffix_len` on one device may be relied on, other than what follows from the above.
Results may differ from the reference program's by a relative error of at most 0.019.
Values may be sent and summed in bfloat16 or wider, within the bound.
A program may use at most 64 MiB of HBM per device.

```python
import math
import jax
import jax.numpy as jnp
import numpy as np
from jax import lax

HEADS = 64
KVH = 8
HD = 128
DOUT = 4096
STEPS = 4
PRE_LEN = 768
SUF_LEN = 64
REQ_DEV = 64
PREFIXES = 64
REQUESTS = 2048
CAP = 2


def draw_queries(key, part):
    key = jax.random.fold_in(key, 11)
    full_shape = (STEPS, REQUESTS, HEADS * HD)
    result_draw = jnp.clip(jax.random.normal(key, full_shape, jnp.float32), -4.5, 4.5)
    return result_draw.astype(jnp.bfloat16)


def draw_new_keys(key, part):
    key = jax.random.fold_in(key, 12)
    full_shape = (STEPS, REQUESTS, KVH * HD)
    result_draw = jnp.clip(jax.random.normal(key, full_shape, jnp.float32), -4.5, 4.5)
    return result_draw.astype(jnp.bfloat16)


def draw_prefix_keys(key, part):
    key = jax.random.fold_in(key, 13)
    full_shape = (PREFIXES, PRE_LEN, KVH * HD)
    result_draw = jnp.clip(jax.random.normal(key, full_shape, jnp.float32), -4.5, 4.5)
    return result_draw.astype(jnp.bfloat16)


def with_spikes(result, own_key, source, target, blocks, factor):
    owner, partner = [(jnp.arange(result.shape[dim]) // (result.shape[dim] // blocks)).reshape([-1 if axis == dim else 1 for axis in range(result.ndim)]) for dim in (source, target)]
    chosen = jax.random.permutation(own_key, blocks)[partner]
    strong = (owner == chosen) | (owner == (partner + blocks // 2) % blocks)
    return jnp.where(strong, factor * result, result)


def shard_levels(stream_key, extent, pieces, low, high):
    def one(position, shards_of):
        steps = jax.random.uniform(jax.random.fold_in(jax.random.fold_in(stream_key, 6), position), (shards_of,), jnp.float32, low / len(pieces), high / len(pieces))
        return jnp.repeat(jnp.exp(steps), extent[position] // shards_of).reshape((-1,) + (1,) * (len(extent) - position - 1))

    gain = one(*pieces[0])
    for cut in pieces[1:]:
        gain = gain * one(*cut)
    return gain


def length_profile(number_of, total, limit, skew):
    portions = [(1 << 20) // math.isqrt(rank ** skew) + 1 for rank in range(2, number_of + 1)]
    surplus, given = total - limit - (number_of - 1), [1] * (number_of - 1)
    while surplus > 0:
        free = [i for i in range(number_of - 1) if given[i] < limit]
        pool, remaining = sum([portions[i] for i in free]), surplus
        for i in free:
            addition = min(limit - given[i], max(1, remaining * portions[i] // pool), surplus)
            given[i] = given[i] + addition
            surplus = surplus - addition
    return np.array([limit] + given)


def ragged_sizes(own_key, amount, total, limit, lean):
    if amount == 2:
        one = jax.random.randint(own_key, (), max(1, total - limit), min(limit, total - 1) + 1)
        return jnp.stack([one, total - one])
    sizes = jnp.asarray(length_profile(amount, total, limit, lean), jnp.int32)
    twos = (amount - 1) // 2
    giver, sink = sizes[1:1 + 2 * twos:2], sizes[2:2 + 2 * twos:2]
    margin = jnp.minimum(giver - 1, limit - sink)
    passed = jax.random.randint(jax.random.fold_in(own_key, 1), (twos,), 0, 1 << 20) % (margin + 1)
    sizes = sizes.at[1:1 + 2 * twos:2].set(giver - passed).at[2:2 + 2 * twos:2].set(sink + passed)
    return sizes[jax.random.permutation(jax.random.fold_in(own_key, 2), amount)]


def assign_block(key, own, number, rows, count, top, reach, skew):
    sequence = jax.random.permutation(key, count)
    crowded, common = load_shares(count, rows * top, reach, skew, True), load_shares(count, rows * top, reach, skew, False)
    places = jnp.arange(count)

    def named(tallies, turn):
        used = int((tallies > 0).sum())
        fixed = max(1, used // 4)
        shifted = fixed + (places - fixed + turn * (used - fixed)) % max(1, count - fixed)
        return jnp.zeros((count,), jnp.int32).at[sequence[jnp.where(places < fixed, places, shifted)]].set(jnp.asarray(tallies, jnp.int32))

    tallies = jnp.where(number % 4 == 0, named(crowded, number // 4), named(common, number - number // 4 - 1))
    mixed = jax.random.permutation(jax.random.fold_in(own, 3), count)
    donor, taker = mixed[0:count // 2 * 2:2], mixed[1:count // 2 * 2:2]
    room = jnp.minimum(tallies[donor] - 1, reach - tallies[taker]) // 2
    room = jnp.where((donor == sequence[0]) | (taker == sequence[0]) | (tallies[taker] == 0), 0, jnp.maximum(room, 0))
    shifted = jax.random.randint(jax.random.fold_in(own, 4), (count // 2,), 0, 1 << 20) % (room + 1)
    tallies = tallies.at[donor].add(-shifted).at[taker].add(shifted)
    members = jnp.searchsorted(jnp.cumsum(tallies), jnp.arange(rows * top), side="right").astype(jnp.int32)
    table = members.reshape(top, rows).T
    table = table[jax.random.permutation(jax.random.fold_in(own, 1), rows)]
    turn = jax.random.randint(jax.random.fold_in(own, 2), (rows, 1), 0, top)
    return jnp.take_along_axis(table, (jnp.arange(top)[None, :] + turn) % top, axis=1)


def load_shares(number_of, total, limit, lean, full):
    loads = [(1 << 20) // math.isqrt(standing ** lean) + 1 for standing in range(1, number_of + 1)]
    largest = limit if full else min(limit, max(-(-total // number_of), total * loads[0] // sum(loads)))
    least = 1 if total - largest >= number_of - 1 else 0
    given, surplus = [largest] + [least] * (number_of - 1), total - largest - least * (number_of - 1)
    while surplus > 0:
        candidates = [i for i in range(1, number_of) if given[i] < largest] or [i for i in range(1, number_of) if given[i] < limit]
        mass, remaining = sum([loads[i] for i in candidates]), surplus
        for i in candidates:
            more = min(limit - given[i], max(1, remaining * loads[i] // mass), surplus)
            given[i] = given[i] + more
            surplus = surplus - more
    return np.array(given)


def scatter_about(own_key, shape, width, reach, shards=(), held_as=jnp.bfloat16):
    values = jax.random.normal(own_key, shape, jnp.float32) * width
    if len(shards) > 0:
        values = shard_levels(own_key, shape, shards, -0.22, 0.18) * values
    return jnp.clip(values, min=-reach, max=reach).astype(held_as)


def gaussian_with(key, extent, scale, most, pieces, heavy, kind=jnp.bfloat16):
    result = scale * jax.random.normal(key, extent, jnp.float32)
    if pieces:
        result = result * shard_levels(key, extent, pieces, -0.22, 0.18)
    return jnp.clip(with_spikes(result, jax.random.fold_in(key, 3), *heavy), -most, most).astype(kind)


def setup_inputs(seed: int = 0) -> dict:
    streams_of = jax.random.split(jax.random.key(seed), 11)
    queries = draw_queries(jax.random.fold_in(streams_of[10], 71), 0)
    new_keys = draw_new_keys(jax.random.fold_in(streams_of[10], 71), 0)
    new_values = scatter_about(streams_of[2], (STEPS, REQUESTS, KVH * HD), 1.0, 4.5, ((1, 32), (2, 8)))
    suffix_keys = scatter_about(streams_of[3], (REQUESTS, SUF_LEN, KVH * HD), 1.0, 4.5, ((0, 32), (2, 8)))
    suffix_values = scatter_about(streams_of[4], (REQUESTS, SUF_LEN, KVH * HD), 1.0, 4.5, ((0, 32), (2, 8)))
    suffix_len = ragged_sizes(streams_of[5], REQUESTS, REQUESTS * SUF_LEN // 2, SUF_LEN, 1).astype(jnp.int32)
    prefix_keys = draw_prefix_keys(jax.random.fold_in(streams_of[10], 71), 0)
    prefix_values = scatter_about(streams_of[7], (PREFIXES, PRE_LEN, KVH * HD), 1.0, 4.5, ((0, 32), (2, 8)))
    prefix_of_keys = jax.random.split(jax.random.fold_in(streams_of[8], 1), REQUESTS // REQ_DEV)
    prefix_of_turns = jax.random.permutation(jax.random.fold_in(streams_of[8], 3), REQUESTS // REQ_DEV)
    prefix_of = jax.vmap(lambda own, number: assign_block(jax.random.fold_in(streams_of[8], 2), own, number, REQ_DEV, PREFIXES, 1, CAP, 2))(prefix_of_keys, prefix_of_turns).reshape((REQUESTS, 1))
    out_weight = gaussian_with(streams_of[9], (HEADS * HD, DOUT), (HEADS * HD) ** -0.5, 0.09375, ((0, 8),), (0, 1, 8, 2.0))
    return dict(queries=queries, new_keys=new_keys, new_values=new_values, suffix_keys=suffix_keys, suffix_values=suffix_values, suffix_len=suffix_len, prefix_keys=prefix_keys, prefix_values=prefix_values, prefix_of=prefix_of, out_weight=out_weight)


def soft_block(scores, value_rows):
    highest = jnp.max(scores, axis=-1, keepdims=True)
    weights = jnp.exp(scores - highest)
    totals = jnp.sum(weights, axis=-1, keepdims=True)
    rounded = lax.optimization_barrier(weights.astype(jnp.bfloat16))
    numerator = jnp.einsum('sgqk,kgd->sgqd', rounded.astype(jnp.float32), value_rows.astype(jnp.float32))
    return numerator / totals, highest[..., 0] + jnp.log(totals[..., 0])


def reference(queries, new_keys, new_values, suffix_keys, suffix_values, suffix_len, prefix_keys, prefix_values, prefix_of, out_weight):
    group_size = HEADS // KVH
    scale = HD ** -0.5
    positions = jnp.arange(SUF_LEN + STEPS, dtype=jnp.int32)
    step_ids = jnp.arange(STEPS, dtype=jnp.int32)

    def one_request(request_item):
        query_rows, fresh_keys, fresh_values, past_keys, past_values, length, owner_id = request_item
        query_heads = query_rows.reshape(STEPS, KVH, group_size, HD).astype(jnp.float32)
        head_keys = lax.dynamic_index_in_dim(prefix_keys, owner_id, 0, keepdims=False).reshape(PRE_LEN, KVH, HD)
        head_values = lax.dynamic_index_in_dim(prefix_values, owner_id, 0, keepdims=False).reshape(PRE_LEN, KVH, HD)
        prefix_scores = jnp.einsum('sgqd,kgd->sgqk', query_heads, head_keys.astype(jnp.float32)) * scale
        prefix_out, prefix_log = soft_block(prefix_scores, head_values)
        local_keys = jnp.concatenate([past_keys, fresh_keys], axis=0).reshape(SUF_LEN + STEPS, KVH, HD)
        local_values = jnp.concatenate([past_values, fresh_values], axis=0).reshape(SUF_LEN + STEPS, KVH, HD)
        local_scores = jnp.einsum('sgqd,kgd->sgqk', query_heads, local_keys.astype(jnp.float32)) * scale
        visible = jnp.where(positions[None, :] < SUF_LEN, positions[None, :] < length, positions[None, :] - SUF_LEN <= step_ids[:, None])
        local_scores = jnp.where(visible[:, None, None, :], local_scores, -jnp.inf)
        local_out, local_log = soft_block(local_scores, local_values)
        highest = jnp.maximum(prefix_log, local_log)
        prefix_weight = jnp.exp(prefix_log - highest)[..., None]
        local_weight = jnp.exp(local_log - highest)[..., None]
        merged = (prefix_weight * prefix_out + local_weight * local_out) / (prefix_weight + local_weight)
        return merged.reshape(STEPS, HEADS * HD).astype(jnp.bfloat16)

    mapped = lax.map(one_request, (queries.transpose(1, 0, 2), new_keys.transpose(1, 0, 2), new_values.transpose(1, 0, 2), suffix_keys, suffix_values, suffix_len, prefix_of[:, 0]))
    attention = mapped.transpose(1, 0, 2).reshape(STEPS * REQUESTS, HEADS * HD)
    projected = jnp.dot(attention, out_weight, preferred_element_type=jnp.float32)
    return projected.astype(jnp.bfloat16).reshape(STEPS, REQUESTS, DOUT)
```

```python
import functools

import jax
import jax.numpy as jnp
from jax import lax
from jax.experimental import pallas as pl
from jax.experimental.pallas import tpu as pltpu
from jax.sharding import PartitionSpec as P

MESH = pl.DeviceIdType.MESH
HD = 128
NZ, NX, NY = 8, 4, 4
NW = NZ * NX
STEPS, REQ, HL = 4, 64, 8
PRE, SUF = 768, 64
ROWS = HL * REQ
SCALE = HD ** (-0.5)
LOG2E = 1.4426950408889634
BLOCK = 8
LKEYS = BLOCK * SUF
DOUT = 4096
SHARE = 512
F32, BF16, I32 = jnp.float32, jnp.bfloat16, jnp.int32


def dot(a, b):
    return lax.dot_general(a, b, (((1,), (0,)), ((), ())), preferred_element_type=F32)


def dot_t(a, b):
    return lax.dot_general(a, b, (((1,), (1,)), ((), ())), preferred_element_type=F32)


def kernel(
    q_hbm, pof_row, pof_col, len_col, nk_hbm, nv_hbm, sk_hbm, sv_hbm, pk_hbm, pv_hbm, w_hbm,
    out_hbm,
    q, nk, nv, sk, sv, pk, pv, w, vones, qf, nkf, nvf, kloc, vloc,
    spread, gather, q_send, q_recv, r_send, r_recv, l_send, l_recv,
    loc_out, loc_log, attn, proj, c_recv, y_send, y_recv, out_v,
    in_sems, out_sems, qs, qr, rs, rr, ls, lr, cs, cr, ys, yr,
):
    me_w, me_t = lax.axis_index("wide"), lax.axis_index("tensor")
    z, x = me_w // NX, me_w % NX
    y, c = me_t // 2, me_t % 2

    def offset(i):
        zi = i // NX
        half = (zi + 1) // 2
        dz = lax.rem(jnp.where(lax.rem(zi, 2) == 1, half, NZ - half), NZ)
        return dz, lax.rem(i, NX)

    def ahead(dz, dx):
        return (lax.rem(z + dz, NZ) * NX + lax.rem(x + dx, NX), me_t)

    def behind(dz, dx):
        return (lax.rem(z + NZ - dz, NZ) * NX + lax.rem(x + NX - dx, NX), me_t)

    def across(dy):
        return (me_w, lax.rem(y + dy, NY) * 2 + c)

    other = (me_w, y * 2 + 1 - c)

    loads = [
        pltpu.make_async_copy(src, dst, in_sems.at[n])
        for n, (src, dst) in enumerate(
            [(q_hbm, q), (pk_hbm, pk), (pv_hbm, pv), (nk_hbm, nk), (nv_hbm, nv),
             (sk_hbm, sk), (sv_hbm, sv), (w_hbm, w)]
        )
    ]
    for load in loads:
        load.start()

    barrier = pltpu.get_barrier_semaphore()

    def greet(i, carry):
        pl.semaphore_signal(barrier, inc=1, device_id=ahead(*offset(i)), device_id_type=MESH)
        return carry

    lax.fori_loop(1, NW, greet, 0)
    for dy in range(1, NY):
        pl.semaphore_signal(barrier, inc=1, device_id=across(dy), device_id_type=MESH)
    pl.semaphore_signal(barrier, inc=1, device_id=other, device_id_type=MESH)

    def slot_of(pof, rank):
        owner = lax.shift_right_logical(pof, 1)
        dz = lax.bitwise_and(lax.shift_right_logical(owner, 2) - z + NZ, NZ - 1)
        dx = lax.bitwise_and(lax.bitwise_and(owner, NX - 1) - x + NX, NX - 1)
        return dz * NX + dx, lax.bitwise_and(pof, 1), rank

    prow = pof_row[...]
    pcol = pof_col[...]
    same = pcol[:REQ] == prow
    before = lax.broadcasted_iota(I32, (REQ, ROWS), 0) < lax.bitwise_and(
        lax.broadcasted_iota(I32, (REQ, ROWS), 1), REQ - 1
    )
    rank_row = jnp.sum(jnp.where(same & before, 1, 0), axis=0, keepdims=True)
    o_row, p_row, k_row = slot_of(prow, rank_row)
    head_row = lax.shift_right_logical(lax.broadcasted_iota(I32, (1, ROWS), 1), 6)
    key_row = (o_row * HL + head_row) * 2 + k_row
    slot_rows = lax.broadcasted_iota(I32, (ROWS, ROWS), 0)
    for p in range(2):
        hit = slot_rows == jnp.where(p_row == p, key_row, -1)
        spread[p] = jnp.where(hit, 1.0, 0.0).astype(BF16)

    loads[0].wait()

    def dispatch(s):
        stacked = jnp.concatenate([q[s, :, h * HD:(h + 1) * HD] for h in range(HL)], axis=0)
        for p in range(2):
            placed = dot(spread[p], stacked).astype(BF16).reshape(NW, 2 * HL, HD)
            q_send[s, :, :, p * HD:(p + 1) * HD] = placed
            q_recv[s, 0, :, p * HD:(p + 1) * HD] = placed[0]

    def send_queries(s):
        def one(i, carry):
            dz, dx = offset(NW - i)
            o = dz * NX + dx
            pltpu.make_async_remote_copy(
                src_ref=q_send.at[s, o], dst_ref=q_recv.at[s, o], send_sem=qs.at[s],
                recv_sem=qr.at[s], device_id=ahead(dz, dx), device_id_type=MESH,
            ).start()
            return carry

        lax.fori_loop(1, NW, one, 0)

    def send_results(s):
        def one(i, carry):
            dz, dx = offset(NW - i)
            o = dz * NX + dx
            pltpu.make_async_remote_copy(
                src_ref=r_send.at[s, o], dst_ref=r_recv.at[s, o], send_sem=rs.at[s],
                recv_sem=rr.at[s], device_id=behind(dz, dx), device_id_type=MESH,
            ).start()
            pltpu.make_async_remote_copy(
                src_ref=l_send.at[s, o], dst_ref=l_recv.at[s, o], send_sem=ls.at[s],
                recv_sem=lr.at[s], device_id=behind(dz, dx), device_id_type=MESH,
            ).start()
            return carry

        lax.fori_loop(1, NW, one, 0)

    def await_all(ref, sem):
        pltpu.make_async_copy(ref, ref, sem).wait()

    dispatch(0)
    pl.semaphore_wait(barrier, NW - 1 + NY - 1 + 1)
    send_queries(0)
    dispatch(1)
    send_queries(1)
    dispatch(2)
    dispatch(3)

    same_c = pcol == prow[:, :REQ]
    before_c = lax.broadcasted_iota(I32, (ROWS, REQ), 1) < lax.bitwise_and(
        lax.broadcasted_iota(I32, (ROWS, REQ), 0), REQ - 1
    )
    rank_col = jnp.sum(jnp.where(same_c & before_c, 1, 0), axis=1, keepdims=True)
    o_col, p_col, k_col = slot_of(pcol, rank_col)
    head_col = lax.shift_right_logical(lax.broadcasted_iota(I32, (ROWS, 1), 0), 6)
    key_col = (o_col * HL + head_col) * 2 + k_col
    slot_cols = lax.broadcasted_iota(I32, (ROWS, ROWS), 1)
    for p in range(2):
        hit = slot_cols == jnp.where(p_col == p, key_col, -1)
        gather[p] = jnp.where(hit, 1.0, 0.0).astype(BF16)
    loads[1].wait()
    loads[2].wait()
    vones[:, :, :HD] = pv[...]
    vones[:, :, HD:] = jnp.ones((2, PRE, HD), BF16)

    for load in loads[3:7]:
        load.wait()
    qf[...] = q[...].astype(F32)
    nkf[...] = nk[...].astype(F32)
    nvf[...] = nv[...].astype(F32)
    kloc[LKEYS:] = jnp.zeros((HD, HD), BF16)
    vloc[LKEYS:, :HD] = jnp.zeros((HD, HD), BF16)
    vloc[:, HD:] = jnp.ones((LKEYS + HD, HD), BF16)
    own_i = lax.broadcasted_iota(I32, (BLOCK, LKEYS), 0)
    own_k = lax.broadcasted_iota(I32, (BLOCK, LKEYS), 1)
    own_hit = lax.shift_right_logical(own_k, 6) == own_i
    own_j = lax.bitwise_and(own_k, SUF - 1)
    new_s = lax.broadcasted_iota(I32, (STEPS, BLOCK, HD), 0)
    new_i = lax.broadcasted_iota(I32, (STEPS, BLOCK, HD), 1)
    new_k = lax.broadcasted_iota(I32, (STEPS, BLOCK, HD), 2)
    new_hit = (lax.bitwise_and(new_k, BLOCK - 1) == new_i) & (
        lax.shift_right_logical(new_k, 3) <= new_s
    )

    def local_block(b, carry):
        rows = pl.ds(pl.multiple_of(b * BLOCK, BLOCK), BLOCK)
        query = jnp.concatenate(
            [qf[s, rows, h * HD:(h + 1) * HD] for s in range(STEPS) for h in range(HL)], axis=0
        ).astype(BF16)
        kloc[:LKEYS] = sk[rows].reshape(LKEYS, HD)
        vloc[:LKEYS, :HD] = sv[rows].reshape(LKEYS, HD)
        kloc[LKEYS:LKEYS + STEPS * BLOCK] = nkf[:, rows, :].reshape(STEPS * BLOCK, HD).astype(BF16)
        vloc[LKEYS:LKEYS + STEPS * BLOCK, :HD] = (
            nvf[:, rows, :].reshape(STEPS * BLOCK, HD).astype(BF16)
        )
        length = len_col[rows, :]
        past = dot_t(query, kloc[:LKEYS]).reshape(STEPS * HL, BLOCK, LKEYS)
        past = jnp.where((own_hit & (own_j < length))[None], past, -jnp.inf)
        fresh = dot_t(query, kloc[LKEYS:]).reshape(STEPS, HL, BLOCK, HD)
        fresh = jnp.where(new_hit[:, None], fresh, -jnp.inf)
        past = past.reshape(STEPS * HL * BLOCK, LKEYS)
        fresh = fresh.reshape(STEPS * HL * BLOCK, HD)
        top = jnp.maximum(
            jnp.max(past, axis=-1, keepdims=True), jnp.max(fresh, axis=-1, keepdims=True)
        )
        past = jnp.exp2((past - top) * (SCALE * LOG2E)).astype(BF16)
        fresh = jnp.exp2((fresh - top) * (SCALE * LOG2E)).astype(BF16)
        both = dot(past, vloc[:LKEYS]) + dot(fresh, vloc[LKEYS:])
        total = both[:, HD:]
        shape = (STEPS, HL, BLOCK, HD)
        loc_out[:, :, rows, :] = (both[:, :HD] / total).reshape(shape)
        loc_log[:, :, rows, :] = (top * SCALE + jnp.log(total)).reshape(shape)
        return carry

    lax.fori_loop(0, REQ // BLOCK, local_block, 0)

    lane = lax.broadcasted_iota(I32, (1, 2 * HL, HD), 2)
    place = lax.broadcasted_iota(I32, (1, 2 * HL, HD), 1)
    PART = 16

    def attend(s):
        await_all(q_recv.at[s, pl.ds(1, NW - 1)], qr.at[s])

        def part(i, carry):
            some = pl.ds(i * PART, PART)
            logs = jnp.zeros((PART, 2 * HL, HD), F32)
            for p in range(2):
                query = q_recv[s, some, :, p * HD:(p + 1) * HD].reshape(PART * 2 * HL, HD)
                scores = dot_t(query, pk[p])
                top = jnp.max(scores, axis=-1, keepdims=True)
                weights = jnp.exp2((scores - top) * (SCALE * LOG2E)).astype(BF16)
                both = dot(weights, vones[p])
                total = both[:, HD:]
                result = (both[:, :HD] / total).astype(BF16)
                r_send[s, some, :, p * HD:(p + 1) * HD] = result.reshape(PART, 2 * HL, HD)
                log = (top * SCALE + jnp.log(total)).reshape(PART, 2 * HL, HD)
                logs = jnp.where(lane == place + p * 2 * HL, log, logs)
            l_send[s, some] = jnp.sum(logs, axis=1, keepdims=True)
            return carry

        lax.fori_loop(0, NW // PART, part, 0)
        r_recv[s, 0] = r_send[s, 0]
        l_recv[s, 0] = l_send[s, 0]
        send_results(s)

    own = jnp.broadcast_to(o_col[:REQ], (REQ, HD))
    pick = p_col[:REQ] * (2 * HL) + k_col[:REQ]
    lanes = lax.broadcasted_iota(I32, (REQ, HD), 1)

    def merge(s):
        await_all(r_recv.at[s, pl.ds(1, NW - 1)], rr.at[s])
        await_all(l_recv.at[s, pl.ds(1, NW - 1)], lr.at[s])
        back = dot(gather[0], r_recv[s, :, :, :HD].reshape(ROWS, HD)) + dot(
            gather[1], r_recv[s, :, :, HD:].reshape(ROWS, HD)
        )
        logs = jnp.zeros((REQ, HD), F32)
        for o in range(NW):
            logs = jnp.where(own == o, l_recv[s, o], logs)
        for h in range(HL):
            pre = jnp.sum(jnp.where(lanes == pick + 2 * h, logs, 0.0), axis=1, keepdims=True)
            loc = loc_log[s, h]
            high = jnp.maximum(pre, loc)
            a, b = jnp.exp(pre - high), jnp.exp(loc - high)
            joint = (a * back[h * REQ:(h + 1) * REQ] + b * loc_out[s, h]) / (a + b)
            attn[s, :, h * HD:(h + 1) * HD] = joint.astype(BF16)
        for dest in range(NY):
            for core in range(2):
                n = (dest * 2 + core) * SHARE
                proj[s, core, dest] = dot(attn[s], w[:, n:n + SHARE]).astype(BF16)
        pltpu.make_async_remote_copy(
            src_ref=proj.at[s, 1 - c], dst_ref=c_recv.at[s], send_sem=cs.at[s],
            recv_sem=cr.at[s], device_id=other, device_id_type=MESH,
        ).start()

    def pair(s):
        await_all(c_recv.at[s], cr.at[s])
        y_send[s] = (proj[s, c].astype(F32) + c_recv[s].astype(F32)).astype(BF16)
        for dy in range(1, NY):
            pltpu.make_async_remote_copy(
                src_ref=y_send.at[s, lax.rem(y + dy, NY)], dst_ref=y_recv.at[s, dy - 1],
                send_sem=ys.at[s], recv_sem=yr.at[s], device_id=across(dy), device_id_type=MESH,
            ).start()

    def finish(s):
        await_all(y_recv.at[s], yr.at[s])
        total = y_send[s, y].astype(F32)
        for dy in range(NY - 1):
            total = total + y_recv[s, dy].astype(F32)
        out_v[s] = total.astype(BF16)
        pltpu.make_async_copy(out_v.at[s], out_hbm.at[s], out_sems.at[s]).start()

    attend(0)
    send_queries(2)
    attend(1)
    send_queries(3)
    loads[7].wait()
    merge(0)
    pair(0)
    attend(2)
    merge(1)
    pair(1)
    finish(0)
    attend(3)
    merge(2)
    pair(2)
    finish(1)
    merge(3)
    pair(3)
    finish(2)
    finish(3)

    for s in range(STEPS):
        await_all(q_send.at[s, pl.ds(1, NW - 1)], qs.at[s])
        await_all(r_send.at[s, pl.ds(1, NW - 1)], rs.at[s])
        await_all(l_send.at[s, pl.ds(1, NW - 1)], ls.at[s])
        await_all(c_recv.at[s], cs.at[s])
        await_all(y_recv.at[s], ys.at[s])
        pltpu.make_async_copy(out_v.at[s], out_hbm.at[s], out_sems.at[s]).wait()


def body(
    queries, new_keys, new_values, suffix_keys, suffix_values, suffix_len,
    prefix_keys, prefix_values, prefix_of, out_weight,
):
    anywhere = pl.BlockSpec(memory_space=pl.ANY)
    vmem = pl.BlockSpec(memory_space=pltpu.VMEM)
    pof = prefix_of[:, 0]
    tiled = jnp.tile(pof, HL)
    dma = pltpu.SemaphoreType.DMA
    slots = (STEPS, NW, 2 * HL, 2 * HD)
    logs = (STEPS, NW, 1, HD)
    return pl.pallas_call(
        kernel,
        out_shape=jax.ShapeDtypeStruct((STEPS, REQ, SHARE), BF16),
        in_specs=[anywhere, vmem, vmem, vmem] + [anywhere] * 7,
        out_specs=anywhere,
        scratch_shapes=[
            pltpu.VMEM(queries.shape, BF16),
            pltpu.VMEM(new_keys.shape, BF16),
            pltpu.VMEM(new_values.shape, BF16),
            pltpu.VMEM(suffix_keys.shape, BF16),
            pltpu.VMEM(suffix_values.shape, BF16),
            pltpu.VMEM(prefix_keys.shape, BF16),
            pltpu.VMEM(prefix_values.shape, BF16),
            pltpu.VMEM(out_weight.shape, BF16),
            pltpu.VMEM((2, PRE, 2 * HD), BF16),
            pltpu.VMEM(queries.shape, F32),
            pltpu.VMEM(new_keys.shape, F32),
            pltpu.VMEM(new_values.shape, F32),
            pltpu.VMEM((LKEYS + HD, HD), BF16),
            pltpu.VMEM((LKEYS + HD, 2 * HD), BF16),
            pltpu.VMEM((2, ROWS, ROWS), BF16),
            pltpu.VMEM((2, ROWS, ROWS), BF16),
            pltpu.VMEM(slots, BF16),
            pltpu.VMEM(slots, BF16),
            pltpu.VMEM(slots, BF16),
            pltpu.VMEM(slots, BF16),
            pltpu.VMEM(logs, F32),
            pltpu.VMEM(logs, F32),
            pltpu.VMEM((STEPS, HL, REQ, HD), F32),
            pltpu.VMEM((STEPS, HL, REQ, HD), F32),
            pltpu.VMEM((STEPS, REQ, HL * HD), BF16),
            pltpu.VMEM((STEPS, 2, NY, REQ, SHARE), BF16),
            pltpu.VMEM((STEPS, NY, REQ, SHARE), BF16),
            pltpu.VMEM((STEPS, NY, REQ, SHARE), BF16),
            pltpu.VMEM((STEPS, NY - 1, REQ, SHARE), BF16),
            pltpu.VMEM((STEPS, REQ, SHARE), BF16),
            dma((8,)),
            dma((STEPS,)),
        ] + [dma((STEPS,))] * 10,
        compiler_params=pltpu.CompilerParams(
            collective_id=0, has_side_effects=True, vmem_limit_bytes=48 * 2**20
        ),
        name="attention",
    )(
        queries, tiled[None, :], tiled[:, None], suffix_len[:, None], new_keys, new_values,
        suffix_keys, suffix_values, prefix_keys, prefix_values, out_weight,
    )


def solution(mesh):
    return jax.shard_map(
        body,
        mesh=mesh,
        in_specs=(
            P(None, "wide", "tensor"),
            P(None, "wide", "tensor"),
            P(None, "wide", "tensor"),
            P("wide", None, "tensor"),
            P("wide", None, "tensor"),
            P("wide"),
            P("wide", None, "tensor"),
            P("wide", None, "tensor"),
            P("wide", None),
            P("tensor", None),
        ),
        out_specs=P(None, "wide", "tensor"),
        check_vma=False,
    )
```

```python
import functools

import jax
import jax.numpy as jnp
from jax import lax
from jax.experimental import pallas as pl
from jax.experimental.pallas import tpu as pltpu
from jax.sharding import PartitionSpec as P

MESH = pl.DeviceIdType.MESH
HD = 128
NZ, NX, NY = 8, 4, 4
NW = NZ * NX
STEPS, REQ, HL = 4, 64, 8
PRE, SUF = 768, 64
ROWS = HL * REQ
SCALE = HD ** (-0.5)
LOG2E = 1.4426950408889634
BLOCK = 8
LKEYS = BLOCK * SUF
DOUT = 4096
SHARE = 512
F32, BF16, I32 = jnp.float32, jnp.bfloat16, jnp.int32


def dot(a, b):
    return lax.dot_general(a, b, (((1,), (0,)), ((), ())), preferred_element_type=F32)


def dot_t(a, b):
    return lax.dot_general(a, b, (((1,), (1,)), ((), ())), preferred_element_type=F32)


def kernel(
    q_hbm, pof_ref, len_ref, nk_hbm, nv_hbm, sk_hbm, sv_hbm, pk_hbm, pv_hbm, w_hbm,
    out_hbm,
    q, nk, nv, sk, sv, pk, pv, w, vones, qf, nkf, nvf, kloc, vloc,
    len_col,
    spread, gather, q_send, q_recv, r_send, r_recv, l_send, l_recv,
    loc_out, loc_log, pre_part, attn, kept, given, c_recv, y_send, y_recv, out_v,
    in_sems, out_sems, qs, qr, rs, rr, ls, lr, cs, cr, ys, yr,
):
    me_w, me_t = lax.axis_index("wide"), lax.axis_index("tensor")
    z, x = me_w // NX, me_w % NX
    y, c = me_t // 2, me_t % 2

    def offset(i):
        zi = i // NX
        half = (zi + 1) // 2
        dz = lax.rem(jnp.where(lax.rem(zi, 2) == 1, half, NZ - half), NZ)
        return dz, lax.rem(i, NX)

    def ahead(dz, dx):
        return (lax.rem(z + dz, NZ) * NX + lax.rem(x + dx, NX), me_t)

    def behind(dz, dx):
        return (lax.rem(z + NZ - dz, NZ) * NX + lax.rem(x + NX - dx, NX), me_t)

    def across(dy):
        return (me_w, lax.rem(y + dy, NY) * 2 + c)

    other = (me_w, y * 2 + 1 - c)

    loads = [
        pltpu.make_async_copy(src, dst, in_sems.at[n])
        for n, (src, dst) in enumerate(
            [(q_hbm, q), (pk_hbm, pk), (pv_hbm, pv), (nk_hbm, nk), (nv_hbm, nv),
             (sk_hbm, sk), (sv_hbm, sv)]
            + [(w_hbm.at[:, pl.ds(n * SHARE, SHARE)], w.at[n]) for n in range(2 * NY)]
        )
    ]
    for load in loads:
        load.start()

    barrier = pltpu.get_barrier_semaphore()

    def greet(i, carry):
        pl.semaphore_signal(barrier, inc=1, device_id=ahead(*offset(i)), device_id_type=MESH)
        return carry

    lax.fori_loop(1, NW, greet, 0)
    for dy in range(1, NY):
        pl.semaphore_signal(barrier, inc=1, device_id=across(dy), device_id_type=MESH)
    pl.semaphore_signal(barrier, inc=1, device_id=other, device_id_type=MESH)

    pof = pof_ref[...]
    sub = lax.broadcasted_iota(I32, (REQ, REQ), 0)
    lane = lax.broadcasted_iota(I32, (REQ, REQ), 1)

    def upright(row):
        return jnp.sum(jnp.where(sub == lane, row, 0), axis=1, keepdims=True)

    rank = jnp.sum(
        jnp.where((upright(pof) == pof) & (sub < lane), 1, 0), axis=0, keepdims=True
    )
    owner = lax.shift_right_logical(pof, 1)
    dz = lax.bitwise_and(lax.shift_right_logical(owner, 2) - z + NZ, NZ - 1)
    dx = lax.bitwise_and(lax.bitwise_and(owner, NX - 1) - x + NX, NX - 1)
    slot = (lax.bitwise_and(pof, 1) * NW + dz * NX + dx) * (2 * HL) + rank
    slot_col = upright(slot)
    wide_sub = lax.broadcasted_iota(I32, (REQ, ROWS), 0)
    wide_lane = lax.broadcasted_iota(I32, (REQ, ROWS), 1)
    key_row = jnp.sum(
        jnp.where(wide_sub == lax.bitwise_and(wide_lane, REQ - 1), slot_col, 0),
        axis=0, keepdims=True,
    ) + 2 * lax.shift_right_logical(lax.broadcasted_iota(I32, (1, ROWS), 1), 6)
    slot_rows = lax.broadcasted_iota(I32, (ROWS, ROWS), 0)
    for p in range(2):
        hit = slot_rows == key_row - p * ROWS
        spread[p] = jnp.where(hit, 1.0, 0.0).astype(BF16)

    loads[0].wait()

    def dispatch(s):
        stacked = jnp.concatenate([q[s, :, h * HD:(h + 1) * HD] for h in range(HL)], axis=0)
        for p in range(2):
            placed = dot(spread[p], stacked).astype(BF16).reshape(NW, 2 * HL, HD)
            q_send[s, :, :, p * HD:(p + 1) * HD] = placed
            q_recv[s, 0, :, p * HD:(p + 1) * HD] = placed[0]

    def send_queries(s):
        def one(i, carry):
            dz, dx = offset(NW - i)
            o = dz * NX + dx
            pltpu.make_async_remote_copy(
                src_ref=q_send.at[s, o], dst_ref=q_recv.at[s, o], send_sem=qs.at[s],
                recv_sem=qr.at[s], device_id=ahead(dz, dx), device_id_type=MESH,
            ).start()
            return carry

        lax.fori_loop(1, NW, one, 0)

    def send_results(s):
        def one(i, carry):
            dz, dx = offset(NW - i)
            o = dz * NX + dx
            pltpu.make_async_remote_copy(
                src_ref=r_send.at[s, o], dst_ref=r_recv.at[s, o], send_sem=rs.at[s],
                recv_sem=rr.at[s], device_id=behind(dz, dx), device_id_type=MESH,
            ).start()
            return carry

        lax.fori_loop(1, NW, one, 0)

    def send_logs(s):
        def one(i, carry):
            dz, dx = offset(NW - i)
            o = dz * NX + dx
            pltpu.make_async_remote_copy(
                src_ref=l_send.at[s, o], dst_ref=l_recv.at[s, o], send_sem=ls.at[s],
                recv_sem=lr.at[s], device_id=behind(dz, dx), device_id_type=MESH,
            ).start()
            return carry

        lax.fori_loop(1, NW, one, 0)

    def await_all(ref, sem):
        pltpu.make_async_copy(ref, ref, sem).wait()

    dispatch(0)
    pl.semaphore_wait(barrier, NW - 1 + NY - 1 + 1)
    send_queries(0)
    dispatch(1)
    send_queries(1)
    dispatch(2)
    dispatch(3)

    tall_sub = lax.broadcasted_iota(I32, (ROWS, REQ), 0)
    tall_lane = lax.broadcasted_iota(I32, (ROWS, REQ), 1)
    key_col = jnp.sum(
        jnp.where(lax.bitwise_and(tall_sub, REQ - 1) == tall_lane, slot, 0),
        axis=1, keepdims=True,
    ) + 2 * lax.shift_right_logical(lax.broadcasted_iota(I32, (ROWS, 1), 0), 6)
    slot_cols = lax.broadcasted_iota(I32, (ROWS, ROWS), 1)
    for p in range(2):
        hit = slot_cols == key_col - p * ROWS
        gather[p] = jnp.where(hit, 1.0, 0.0).astype(BF16)
    len_col[...] = jnp.broadcast_to(upright(len_ref[...]), (REQ, HD))
    loads[1].wait()
    loads[2].wait()
    vones[:, :, :HD] = pv[...]
    vones[:, :, HD:] = jnp.ones((2, PRE, HD), BF16)

    for load in loads[3:7]:
        load.wait()
    qf[...] = q[...].astype(F32)
    nkf[...] = nk[...].astype(F32)
    nvf[...] = nv[...].astype(F32)
    kloc[LKEYS:] = jnp.zeros((HD, HD), BF16)
    vloc[LKEYS:, :HD] = jnp.zeros((HD, HD), BF16)
    vloc[:, HD:] = jnp.ones((LKEYS + HD, HD), BF16)
    own_i = lax.broadcasted_iota(I32, (BLOCK, LKEYS), 0)
    own_k = lax.broadcasted_iota(I32, (BLOCK, LKEYS), 1)
    own_hit = lax.shift_right_logical(own_k, 6) == own_i
    own_j = lax.bitwise_and(own_k, SUF - 1)
    new_s = lax.broadcasted_iota(I32, (STEPS, BLOCK, HD), 0)
    new_i = lax.broadcasted_iota(I32, (STEPS, BLOCK, HD), 1)
    new_k = lax.broadcasted_iota(I32, (STEPS, BLOCK, HD), 2)
    new_hit = (lax.bitwise_and(new_k, BLOCK - 1) == new_i) & (
        lax.shift_right_logical(new_k, 3) <= new_s
    )

    def local_block(b, carry):
        rows = pl.ds(pl.multiple_of(b * BLOCK, BLOCK), BLOCK)
        query = jnp.concatenate(
            [qf[s, rows, h * HD:(h + 1) * HD] for s in range(STEPS) for h in range(HL)], axis=0
        ).astype(BF16)
        kloc[:LKEYS] = sk[rows].reshape(LKEYS, HD)
        vloc[:LKEYS, :HD] = sv[rows].reshape(LKEYS, HD)
        kloc[LKEYS:LKEYS + STEPS * BLOCK] = nkf[:, rows, :].reshape(STEPS * BLOCK, HD).astype(BF16)
        vloc[LKEYS:LKEYS + STEPS * BLOCK, :HD] = (
            nvf[:, rows, :].reshape(STEPS * BLOCK, HD).astype(BF16)
        )
        length = len_col[rows, :1]
        past = dot_t(query, kloc[:LKEYS]).reshape(STEPS * HL, BLOCK, LKEYS)
        past = jnp.where((own_hit & (own_j < length))[None], past, -jnp.inf)
        fresh = dot_t(query, kloc[LKEYS:]).reshape(STEPS, HL, BLOCK, HD)
        fresh = jnp.where(new_hit[:, None], fresh, -jnp.inf)
        past = past.reshape(STEPS * HL * BLOCK, LKEYS)
        fresh = fresh.reshape(STEPS * HL * BLOCK, HD)
        top = jnp.maximum(
            jnp.max(past, axis=-1, keepdims=True), jnp.max(fresh, axis=-1, keepdims=True)
        )
        past = jnp.exp2((past - top) * (SCALE * LOG2E)).astype(BF16)
        fresh = jnp.exp2((fresh - top) * (SCALE * LOG2E)).astype(BF16)
        both = dot(past, vloc[:LKEYS]) + dot(fresh, vloc[LKEYS:])
        total = both[:, HD:]
        shape = (STEPS, HL, BLOCK, HD)
        loc_out[:, :, rows, :] = (both[:, :HD] / total).reshape(shape)
        loc_log[:, :, rows, :] = (top * SCALE + jnp.log(total)).reshape(shape)
        return carry

    lax.fori_loop(0, REQ // BLOCK, local_block, 0)

    log_lane = lax.broadcasted_iota(I32, (1, 2 * HL, HD), 2)
    place = lax.broadcasted_iota(I32, (1, 2 * HL, HD), 1)
    PART = 16

    def attend(s):
        await_all(q_recv.at[s, pl.ds(1, NW - 1)], qr.at[s])

        def part(i, carry):
            some = pl.ds(i * PART, PART)
            logs = jnp.zeros((PART, 2 * HL, HD), F32)
            for p in range(2):
                query = q_recv[s, some, :, p * HD:(p + 1) * HD].reshape(PART * 2 * HL, HD)
                scores = dot_t(query, pk[p])
                top = jnp.max(scores, axis=-1, keepdims=True)
                weights = jnp.exp2((scores - top) * (SCALE * LOG2E)).astype(BF16)
                both = dot(weights, vones[p])
                total = both[:, HD:]
                result = (both[:, :HD] / total).astype(BF16)
                r_send[s, some, :, p * HD:(p + 1) * HD] = result.reshape(PART, 2 * HL, HD)
                log = (top * SCALE + jnp.log(total)).reshape(PART, 2 * HL, HD)
                logs = jnp.where(log_lane == place + p * 2 * HL, log, logs)
            l_send[s, some] = jnp.sum(logs, axis=1, keepdims=True)
            return carry

        lax.fori_loop(0, NW // PART, part, 0)
        r_recv[s, 0] = r_send[s, 0]
        l_recv[s, 0] = l_send[s, 0]
        send_logs(s)
        send_results(s)

    own = jnp.broadcast_to(
        lax.bitwise_and(lax.shift_right_logical(slot_col, 4), NW - 1), (REQ, HD)
    )
    pick = lax.shift_right_logical(slot_col, 9) * (2 * HL) + lax.bitwise_and(slot_col, 1)
    lanes = lax.broadcasted_iota(I32, (REQ, HD), 1)

    def merge(s):
        await_all(l_recv.at[s, pl.ds(1, NW - 1)], lr.at[s])
        logs = jnp.zeros((REQ, HD), F32)
        for o in range(NW):
            logs = jnp.where(own == o, l_recv[s, o], logs)
        for h in range(HL):
            pre = jnp.sum(jnp.where(lanes == pick + 2 * h, logs, 0.0), axis=1, keepdims=True)
            loc = loc_log[s, h]
            high = jnp.maximum(pre, loc)
            a, b = jnp.exp(pre - high), jnp.exp(loc - high)
            pre_part[h] = a / (a + b)
            loc_out[s, h] = loc_out[s, h] * (b / (a + b))
        await_all(r_recv.at[s, pl.ds(1, NW - 1)], rr.at[s])
        back = dot(gather[0], r_recv[s, :, :, :HD].reshape(ROWS, HD)) + dot(
            gather[1], r_recv[s, :, :, HD:].reshape(ROWS, HD)
        )
        for h in range(HL):
            joint = pre_part[h] * back[h * REQ:(h + 1) * REQ] + loc_out[s, h]
            attn[s, :, h * HD:(h + 1) * HD] = joint.astype(BF16)

    def block(dy, core):
        return lax.rem(y + dy, NY) * 2 + core

    def give(s, dy):
        given[s, dy] = dot(attn[s], w[block(dy, 1 - c)]).astype(BF16)
        pltpu.make_async_remote_copy(
            src_ref=given.at[s, dy], dst_ref=c_recv.at[s, dy], send_sem=cs.at[s, dy],
            recv_sem=cr.at[s, dy], device_id=other, device_id_type=MESH,
        ).start()

    def keep(s, dy):
        kept[s, dy] = dot(attn[s], w[block(dy, c)])

    def pair(s, dy):
        await_all(c_recv.at[s, dy], cr.at[s, dy])
        both = kept[s, dy] + c_recv[s, dy].astype(F32)
        if dy == 0:
            kept[s, dy] = both
            return
        y_send[s, dy - 1] = both.astype(BF16)
        pltpu.make_async_remote_copy(
            src_ref=y_send.at[s, dy - 1], dst_ref=y_recv.at[s, dy - 1],
            send_sem=ys.at[s], recv_sem=yr.at[s], device_id=across(dy), device_id_type=MESH,
        ).start()

    def project(s):
        give(s, 2)
        give(s, 1)
        give(s, 3)
        keep(s, 2)
        keep(s, 1)
        pair(s, 2)
        keep(s, 3)
        pair(s, 1)
        give(s, 0)
        pair(s, 3)
        keep(s, 0)
        pair(s, 0)

    def finish(s):
        await_all(y_recv.at[s], yr.at[s])
        total = kept[s, 0]
        for dy in range(NY - 1):
            total = total + y_recv[s, dy].astype(F32)
        out_v[s] = total.astype(BF16)
        pltpu.make_async_copy(out_v.at[s], out_hbm.at[s], out_sems.at[s]).start()

    attend(0)
    send_queries(2)
    attend(1)
    send_queries(3)
    for load in loads[7:]:
        load.wait()
    merge(0)
    project(0)
    attend(2)
    merge(1)
    project(1)
    finish(0)
    attend(3)
    merge(2)
    project(2)
    finish(1)
    merge(3)
    project(3)
    finish(2)
    finish(3)

    for s in range(STEPS):
        await_all(q_send.at[s, pl.ds(1, NW - 1)], qs.at[s])
        await_all(r_send.at[s, pl.ds(1, NW - 1)], rs.at[s])
        await_all(l_send.at[s, pl.ds(1, NW - 1)], ls.at[s])
        for dy in range(NY):
            await_all(given.at[s, dy], cs.at[s, dy])
        await_all(y_send.at[s], ys.at[s])
        pltpu.make_async_copy(out_v.at[s], out_hbm.at[s], out_sems.at[s]).wait()


def body(
    queries, new_keys, new_values, suffix_keys, suffix_values, suffix_len,
    prefix_keys, prefix_values, prefix_of, out_weight,
):
    anywhere = pl.BlockSpec(memory_space=pl.ANY)
    vmem = pl.BlockSpec(memory_space=pltpu.VMEM)
    dma = pltpu.SemaphoreType.DMA
    slots = (STEPS, NW, 2 * HL, 2 * HD)
    logs = (STEPS, NW, 1, HD)
    return pl.pallas_call(
        kernel,
        out_shape=jax.ShapeDtypeStruct((STEPS, REQ, SHARE), BF16),
        in_specs=[anywhere, vmem, vmem] + [anywhere] * 7,
        out_specs=anywhere,
        scratch_shapes=[
            pltpu.VMEM(queries.shape, BF16),
            pltpu.VMEM(new_keys.shape, BF16),
            pltpu.VMEM(new_values.shape, BF16),
            pltpu.VMEM(suffix_keys.shape, BF16),
            pltpu.VMEM(suffix_values.shape, BF16),
            pltpu.VMEM(prefix_keys.shape, BF16),
            pltpu.VMEM(prefix_values.shape, BF16),
            pltpu.VMEM((2 * NY, out_weight.shape[0], SHARE), BF16),
            pltpu.VMEM((2, PRE, 2 * HD), BF16),
            pltpu.VMEM(queries.shape, F32),
            pltpu.VMEM(new_keys.shape, F32),
            pltpu.VMEM(new_values.shape, F32),
            pltpu.VMEM((LKEYS + HD, HD), BF16),
            pltpu.VMEM((LKEYS + HD, 2 * HD), BF16),
            pltpu.VMEM((REQ, HD), I32),
            pltpu.VMEM((2, ROWS, ROWS), BF16),
            pltpu.VMEM((2, ROWS, ROWS), BF16),
            pltpu.VMEM(slots, BF16),
            pltpu.VMEM(slots, BF16),
            pltpu.VMEM(slots, BF16),
            pltpu.VMEM(slots, BF16),
            pltpu.VMEM(logs, F32),
            pltpu.VMEM(logs, F32),
            pltpu.VMEM((STEPS, HL, REQ, HD), F32),
            pltpu.VMEM((STEPS, HL, REQ, HD), F32),
            pltpu.VMEM((HL, REQ, HD), F32),
            pltpu.VMEM((STEPS, REQ, HL * HD), BF16),
            pltpu.VMEM((STEPS, NY, REQ, SHARE), F32),
            pltpu.VMEM((STEPS, NY, REQ, SHARE), BF16),
            pltpu.VMEM((STEPS, NY, REQ, SHARE), BF16),
            pltpu.VMEM((STEPS, NY - 1, REQ, SHARE), BF16),
            pltpu.VMEM((STEPS, NY - 1, REQ, SHARE), BF16),
            pltpu.VMEM((STEPS, REQ, SHARE), BF16),
            dma((7 + 2 * NY,)),
            dma((STEPS,)),
        ] + [dma((STEPS,))] * 6 + [dma((STEPS, NY))] * 2 + [dma((STEPS,))] * 2,
        compiler_params=pltpu.CompilerParams(
            collective_id=0, has_side_effects=True, vmem_limit_bytes=62 * 2**20
        ),
        name="attention",
    )(
        queries, prefix_of.reshape(1, REQ), suffix_len.reshape(1, REQ), new_keys, new_values,
        suffix_keys, suffix_values, prefix_keys, prefix_values, out_weight,
    )


def solution(mesh):
    return jax.shard_map(
        body,
        mesh=mesh,
        in_specs=(
            P(None, "wide", "tensor"),
            P(None, "wide", "tensor"),
            P(None, "wide", "tensor"),
            P("wide", None, "tensor"),
            P("wide", None, "tensor"),
            P("wide"),
            P("wide", None, "tensor"),
            P("wide", None, "tensor"),
            P("wide", None),
            P("tensor", None),
        ),
        out_specs=P(None, "wide", "tensor"),
        check_vma=False,
    )
```

```python
import functools

import jax
import jax.numpy as jnp
from jax import lax
from jax.experimental import pallas as pl
from jax.experimental.pallas import tpu as pltpu
from jax.sharding import PartitionSpec as P

MESH = pl.DeviceIdType.MESH
HD = 128
NZ, NX, NY = 8, 4, 4
NW = NZ * NX
STEPS, REQ, HL = 4, 64, 8
PRE, SUF = 768, 64
ROWS = HL * REQ
HALF = ROWS // 2
LAST = STEPS - 1
SCALE = HD ** (-0.5)
LOG2E = 1.4426950408889634
BLOCK = 8
LKEYS = BLOCK * SUF
DOUT = 4096
SHARE = 512
F32, BF16, I32 = jnp.float32, jnp.bfloat16, jnp.int32


def dot(a, b):
    return lax.dot_general(a, b, (((1,), (0,)), ((), ())), preferred_element_type=F32)


def dot_t(a, b):
    return lax.dot_general(a, b, (((1,), (1,)), ((), ())), preferred_element_type=F32)


def kernel(
    q_hbm, pof_ref, len_ref, nk_hbm, nv_hbm, sk_hbm, sv_hbm, pk_hbm, pv_hbm, w_hbm,
    own_hbm, y_recv,
    q, nk, nv, sk, sv, pk, pv, w, vones, qf, nkf, nvf, kloc, vloc,
    len_col,
    spread, gather, q_send, q_recv, r_send, r_recv, l_send, l_recv,
    loc_out, loc_log, pre_part, attn, early, kept, given, c_recv, y_send,
    in_sems, out_sems, qs, qr, rs, rr, ls, lr, cs, cr, ys, yr,
):
    me_w, me_t = lax.axis_index("wide"), lax.axis_index("tensor")
    z, x = me_w // NX, me_w % NX
    y, c = me_t // 2, me_t % 2

    def offset(i):
        zi = i // NX
        half = (zi + 1) // 2
        dz = lax.rem(jnp.where(lax.rem(zi, 2) == 1, half, NZ - half), NZ)
        return dz, lax.rem(i, NX)

    def ahead(dz, dx):
        return (lax.rem(z + dz, NZ) * NX + lax.rem(x + dx, NX), me_t)

    def behind(dz, dx):
        return (lax.rem(z + NZ - dz, NZ) * NX + lax.rem(x + NX - dx, NX), me_t)

    def across(dy):
        return (me_w, lax.rem(y + dy, NY) * 2 + c)

    other = (me_w, y * 2 + 1 - c)

    loads = [
        pltpu.make_async_copy(src, dst, in_sems.at[n])
        for n, (src, dst) in enumerate(
            [(q_hbm.at[s], q.at[s]) for s in range(STEPS)]
            + [(pk_hbm, pk), (pv_hbm, pv), (nk_hbm, nk), (nv_hbm, nv), (sk_hbm, sk), (sv_hbm, sv)]
            + [(w_hbm.at[:, pl.ds(n * SHARE, SHARE)], w.at[n]) for n in range(2 * NY)]
        )
    ]
    for load in loads[:STEPS]:
        load.start()

    barrier = pltpu.get_barrier_semaphore()

    def greet(i, carry):
        pl.semaphore_signal(barrier, inc=1, device_id=ahead(*offset(i)), device_id_type=MESH)
        return carry

    lax.fori_loop(1, NW, greet, 0)
    for dy in range(1, NY):
        pl.semaphore_signal(barrier, inc=1, device_id=across(dy), device_id_type=MESH)
    pl.semaphore_signal(barrier, inc=1, device_id=other, device_id_type=MESH)

    pof = pof_ref[...]
    sub = lax.broadcasted_iota(I32, (REQ, REQ), 0)
    lane = lax.broadcasted_iota(I32, (REQ, REQ), 1)

    def upright(row):
        return jnp.sum(jnp.where(sub == lane, row, 0), axis=1, keepdims=True)

    rank = jnp.sum(
        jnp.where((upright(pof) == pof) & (sub < lane), 1, 0), axis=0, keepdims=True
    )
    owner = lax.shift_right_logical(pof, 1)
    dz = lax.bitwise_and(lax.shift_right_logical(owner, 2) - z + NZ, NZ - 1)
    dx = lax.bitwise_and(lax.bitwise_and(owner, NX - 1) - x + NX, NX - 1)
    slot = (dz * NX + dx) * 16 + lax.bitwise_and(pof, 1) * 8 + rank
    slot_col = upright(slot)
    wide_sub = lax.broadcasted_iota(I32, (REQ, HALF), 0)
    wide_lane = lax.broadcasted_iota(I32, (REQ, HALF), 1)
    key_row = jnp.sum(
        jnp.where(wide_sub == lax.bitwise_and(wide_lane, REQ - 1), slot_col, 0),
        axis=0, keepdims=True,
    ) + 2 * lax.shift_right_logical(lax.broadcasted_iota(I32, (1, HALF), 1), 6)
    hit = lax.broadcasted_iota(I32, (ROWS, HALF), 0) == key_row
    spread[...] = jnp.where(hit, 1.0, 0.0).astype(BF16)

    def dispatch(s):
        loads[s].wait()
        for half in range(2):
            stacked = jnp.concatenate(
                [q[s, :, h * HD:(h + 1) * HD] for h in range(half * 4, half * 4 + 4)], axis=0
            )
            placed = dot(spread[...], stacked).astype(BF16).reshape(NW, 16, HD)
            q_send[s, :, half] = placed
            q_recv[s, 0, half] = placed[0]

    def send_queries(s):
        def one(i, carry):
            dz, dx = offset(NW - i)
            o = dz * NX + dx
            pltpu.make_async_remote_copy(
                src_ref=q_send.at[s, o], dst_ref=q_recv.at[s, o], send_sem=qs.at[s],
                recv_sem=qr.at[s], device_id=ahead(dz, dx), device_id_type=MESH,
            ).start()
            return carry

        lax.fori_loop(1, NW, one, 0)

    def send_results(s, half=None):
        part = pl.ds(0, 2) if half is None else pl.ds(half, 1)

        def one(i, carry):
            dz, dx = offset(NW - i)
            o = dz * NX + dx
            pltpu.make_async_remote_copy(
                src_ref=r_send.at[s, o, part], dst_ref=r_recv.at[s, o, part],
                send_sem=rs.at[s + (half or 0)], recv_sem=rr.at[s + (half or 0)],
                device_id=behind(dz, dx), device_id_type=MESH,
            ).start()
            return carry

        lax.fori_loop(1, NW, one, 0)

    def send_logs(s):
        def one(i, carry):
            dz, dx = offset(NW - i)
            o = dz * NX + dx
            pltpu.make_async_remote_copy(
                src_ref=l_send.at[s, o], dst_ref=l_recv.at[s, o], send_sem=ls.at[s],
                recv_sem=lr.at[s], device_id=behind(dz, dx), device_id_type=MESH,
            ).start()
            return carry

        lax.fori_loop(1, NW, one, 0)

    def await_all(ref, sem):
        pltpu.make_async_copy(ref, ref, sem).wait()

    dispatch(0)
    pl.semaphore_wait(barrier, NW - 1 + NY - 1 + 1)
    send_queries(0)
    for load in loads[STEPS:]:
        load.start()
    dispatch(1)
    send_queries(1)
    dispatch(2)
    send_queries(2)
    dispatch(3)

    tall_sub = lax.broadcasted_iota(I32, (HALF, REQ), 0)
    tall_lane = lax.broadcasted_iota(I32, (HALF, REQ), 1)
    key_col = jnp.sum(
        jnp.where(lax.bitwise_and(tall_sub, REQ - 1) == tall_lane, slot, 0),
        axis=1, keepdims=True,
    ) + 2 * lax.shift_right_logical(lax.broadcasted_iota(I32, (HALF, 1), 0), 6)
    hit = lax.broadcasted_iota(I32, (HALF, ROWS), 1) == key_col
    gather[...] = jnp.where(hit, 1.0, 0.0).astype(BF16)
    len_col[...] = jnp.broadcast_to(upright(len_ref[...]), (REQ, HD))
    loads[4].wait()
    loads[5].wait()
    vones[:, :, :HD] = pv[...]
    vones[:, :, HD:] = jnp.ones((2, PRE, HD), BF16)

    for load in loads[6:10]:
        load.wait()
    qf[...] = q[...].astype(F32)
    nkf[...] = nk[...].astype(F32)
    nvf[...] = nv[...].astype(F32)
    kloc[LKEYS:] = jnp.zeros((HD, HD), BF16)
    vloc[LKEYS:, :HD] = jnp.zeros((HD, HD), BF16)
    vloc[:, HD:] = jnp.ones((LKEYS + HD, HD), BF16)
    own_i = lax.broadcasted_iota(I32, (BLOCK, LKEYS), 0)
    own_k = lax.broadcasted_iota(I32, (BLOCK, LKEYS), 1)
    own_hit = lax.shift_right_logical(own_k, 6) == own_i
    own_j = lax.bitwise_and(own_k, SUF - 1)
    new_s = lax.broadcasted_iota(I32, (STEPS, BLOCK, HD), 0)
    new_i = lax.broadcasted_iota(I32, (STEPS, BLOCK, HD), 1)
    new_k = lax.broadcasted_iota(I32, (STEPS, BLOCK, HD), 2)
    new_hit = (lax.bitwise_and(new_k, BLOCK - 1) == new_i) & (
        lax.shift_right_logical(new_k, 3) <= new_s
    )

    def local_block(b, carry):
        rows = pl.ds(pl.multiple_of(b * BLOCK, BLOCK), BLOCK)
        query = jnp.concatenate(
            [qf[s, rows, h * HD:(h + 1) * HD] for s in range(STEPS) for h in range(HL)], axis=0
        ).astype(BF16)
        kloc[:LKEYS] = sk[rows].reshape(LKEYS, HD)
        vloc[:LKEYS, :HD] = sv[rows].reshape(LKEYS, HD)
        kloc[LKEYS:LKEYS + STEPS * BLOCK] = nkf[:, rows, :].reshape(STEPS * BLOCK, HD).astype(BF16)
        vloc[LKEYS:LKEYS + STEPS * BLOCK, :HD] = (
            nvf[:, rows, :].reshape(STEPS * BLOCK, HD).astype(BF16)
        )
        length = len_col[rows, :1]
        past = dot_t(query, kloc[:LKEYS]).reshape(STEPS * HL, BLOCK, LKEYS)
        past = jnp.where((own_hit & (own_j < length))[None], past, -jnp.inf)
        fresh = dot_t(query, kloc[LKEYS:]).reshape(STEPS, HL, BLOCK, HD)
        fresh = jnp.where(new_hit[:, None], fresh, -jnp.inf)
        past = past.reshape(STEPS * HL * BLOCK, LKEYS)
        fresh = fresh.reshape(STEPS * HL * BLOCK, HD)
        top = jnp.maximum(
            jnp.max(past, axis=-1, keepdims=True), jnp.max(fresh, axis=-1, keepdims=True)
        )
        past = jnp.exp2((past - top) * (SCALE * LOG2E)).astype(BF16)
        fresh = jnp.exp2((fresh - top) * (SCALE * LOG2E)).astype(BF16)
        both = dot(past, vloc[:LKEYS]) + dot(fresh, vloc[LKEYS:])
        total = both[:, HD:]
        shape = (STEPS, HL, BLOCK, HD)
        loc_out[:, :, rows, :] = (both[:, :HD] / total).reshape(shape)
        loc_log[:, :, rows, :] = (top * SCALE + jnp.log(total)).reshape(shape)
        return carry

    lax.fori_loop(0, REQ // BLOCK, local_block, 0)

    log_lane = lax.broadcasted_iota(I32, (1, 2 * HL, HD), 2)
    place = lax.broadcasted_iota(I32, (1, 2 * HL, HD), 1)
    PART = 16

    def attend(s):
        await_all(q_recv.at[s, pl.ds(1, NW - 1)], qr.at[s])

        def part(i, carry):
            some = pl.ds(i * PART, PART)
            logs = jnp.zeros((PART, 2 * HL, HD), F32)
            arrived = q_recv[s, some].astype(F32)
            results = []
            for p in range(2):
                rows = slice(p * 8, p * 8 + 8)
                query = jnp.concatenate([arrived[:, 0, rows], arrived[:, 1, rows]], axis=1)
                scores = dot_t(query.astype(BF16).reshape(PART * 2 * HL, HD), pk[p])
                top = jnp.max(scores, axis=-1, keepdims=True)
                weights = jnp.exp2((scores - top) * (SCALE * LOG2E)).astype(BF16)
                both = dot(weights, vones[p])
                total = both[:, HD:]
                results.append((both[:, :HD] / total).reshape(PART, 2 * HL, HD))
                log = (top * SCALE + jnp.log(total)).reshape(PART, 2 * HL, HD)
                logs = jnp.where(log_lane == place + p * 2 * HL, log, logs)
            for half in range(2):
                rows = slice(half * 8, half * 8 + 8)
                r_send[s, some, half] = jnp.concatenate(
                    [results[0][:, rows], results[1][:, rows]], axis=1
                ).astype(BF16)
            l_send[s, some] = jnp.sum(logs, axis=1, keepdims=True)
            return carry

        lax.fori_loop(0, NW // PART, part, 0)
        r_recv[s, 0] = r_send[s, 0]
        l_recv[s, 0] = l_send[s, 0]
        send_logs(s)
        if s == LAST:
            send_results(s, 0)
            send_results(s, 1)
        else:
            send_results(s)

    own = jnp.broadcast_to(lax.shift_right_logical(slot_col, 4), (REQ, HD))
    pick = lax.bitwise_and(slot_col, 8) * 2 + lax.bitwise_and(slot_col, 1)
    lanes = lax.broadcasted_iota(I32, (REQ, HD), 1)

    def merge(s):
        await_all(l_recv.at[s, pl.ds(1, NW - 1)], lr.at[s])
        logs = jnp.zeros((REQ, HD), F32)
        for o in range(NW):
            logs = jnp.where(own == o, l_recv[s, o], logs)
        for h in range(HL):
            pre = jnp.sum(jnp.where(lanes == pick + 2 * h, logs, 0.0), axis=1, keepdims=True)
            loc = loc_log[s, h]
            high = jnp.maximum(pre, loc)
            a, b = jnp.exp(pre - high), jnp.exp(loc - high)
            pre_part[h] = a / (a + b)
            loc_out[s, h] = loc_out[s, h] * (b / (a + b))

    def take(s, half):
        back = dot(gather[...], r_recv[s, :, half].reshape(ROWS, HD))
        for n in range(4):
            h = half * 4 + n
            joint = pre_part[h] * back[n * REQ:(n + 1) * REQ] + loc_out[s, h]
            attn[s, :, h * HD:(h + 1) * HD] = joint.astype(BF16)

    def block(dy, core):
        return lax.rem(y + dy, NY) * 2 + core

    WIDE = HL * HD // 2

    def term(s, dy, side):
        n = block(dy, 1 - c if side else c)
        if s == LAST:
            return early[dy, side] + dot(attn[s, :, WIDE:], w[n, WIDE:])
        return dot(attn[s], w[n])

    def begin(s):
        for side in (1, 0):
            for dy in (2, 1, 3, 0):
                n = block(dy, 1 - c if side else c)
                early[dy, side] = dot(attn[s, :, :WIDE], w[n, :WIDE])

    def give(s, dy):
        given[s, dy] = term(s, dy, 1).astype(BF16)
        pltpu.make_async_remote_copy(
            src_ref=given.at[s, dy], dst_ref=c_recv.at[s, dy], send_sem=cs.at[s, dy],
            recv_sem=cr.at[s, dy], device_id=other, device_id_type=MESH,
        ).start()

    def keep(s, dy):
        kept[s, dy] = term(s, dy, 0)

    def pair(s, dy):
        await_all(c_recv.at[s, dy], cr.at[s, dy])
        both = kept[s, dy] + c_recv[s, dy].astype(F32)
        if dy == 0:
            kept[s, dy] = both
            pltpu.make_async_copy(kept.at[s, dy], own_hbm.at[s], out_sems.at[s]).start()
            return
        y_send[s, dy - 1] = both.astype(BF16)
        pltpu.make_async_remote_copy(
            src_ref=y_send.at[s, dy - 1], dst_ref=y_recv.at[s, dy - 1],
            send_sem=ys.at[s], recv_sem=yr.at[s], device_id=across(dy), device_id_type=MESH,
        ).start()

    def project(s):
        give(s, 2)
        give(s, 1)
        give(s, 3)
        keep(s, 2)
        keep(s, 1)
        pair(s, 2)
        keep(s, 3)
        pair(s, 1)
        give(s, 0)
        pair(s, 3)
        keep(s, 0)
        pair(s, 0)

    def step(s):
        merge(s)
        if s == LAST:
            for half in range(2):
                await_all(r_recv.at[s, pl.ds(1, NW - 1), half], rr.at[s + half])
                take(s, half)
                if half == 0:
                    begin(s)
        else:
            await_all(r_recv.at[s, pl.ds(1, NW - 1)], rr.at[s])
            take(s, 0)
            take(s, 1)
        project(s)

    attend(0)
    send_queries(3)
    attend(1)
    attend(2)
    for load in loads[10:]:
        load.wait()
    step(0)
    attend(3)
    for s in range(1, STEPS):
        step(s)

    for s in range(STEPS):
        await_all(q_send.at[s, pl.ds(1, NW - 1)], qs.at[s])
        if s == LAST:
            for half in range(2):
                await_all(r_send.at[s, pl.ds(1, NW - 1), half], rs.at[s + half])
        else:
            await_all(r_send.at[s, pl.ds(1, NW - 1)], rs.at[s])
        await_all(l_send.at[s, pl.ds(1, NW - 1)], ls.at[s])
        for dy in range(NY):
            await_all(given.at[s, dy], cs.at[s, dy])
        await_all(y_send.at[s], ys.at[s])
        pltpu.make_async_copy(kept.at[s, 0], own_hbm.at[s], out_sems.at[s]).wait()
    for s in range(STEPS):
        await_all(y_recv.at[s], yr.at[s])


def body(
    queries, new_keys, new_values, suffix_keys, suffix_values, suffix_len,
    prefix_keys, prefix_values, prefix_of, out_weight,
):
    anywhere = pl.BlockSpec(memory_space=pl.ANY)
    vmem = pl.BlockSpec(memory_space=pltpu.VMEM)
    dma = pltpu.SemaphoreType.DMA
    slots = (STEPS, NW, 2, 16, HD)
    logs = (STEPS, NW, 1, HD)
    own, parts = pl.pallas_call(
        kernel,
        out_shape=(
            jax.ShapeDtypeStruct((STEPS, REQ, SHARE), F32),
            jax.ShapeDtypeStruct((STEPS, NY - 1, REQ, SHARE), BF16),
        ),
        in_specs=[anywhere, vmem, vmem] + [anywhere] * 7,
        out_specs=(anywhere, anywhere),
        scratch_shapes=[
            pltpu.VMEM(queries.shape, BF16),
            pltpu.VMEM(new_keys.shape, BF16),
            pltpu.VMEM(new_values.shape, BF16),
            pltpu.VMEM(suffix_keys.shape, BF16),
            pltpu.VMEM(suffix_values.shape, BF16),
            pltpu.VMEM(prefix_keys.shape, BF16),
            pltpu.VMEM(prefix_values.shape, BF16),
            pltpu.VMEM((2 * NY, out_weight.shape[0], SHARE), BF16),
            pltpu.VMEM((2, PRE, 2 * HD), BF16),
            pltpu.VMEM(queries.shape, F32),
            pltpu.VMEM(new_keys.shape, F32),
            pltpu.VMEM(new_values.shape, F32),
            pltpu.VMEM((LKEYS + HD, HD), BF16),
            pltpu.VMEM((LKEYS + HD, 2 * HD), BF16),
            pltpu.VMEM((REQ, HD), I32),
            pltpu.VMEM((ROWS, HALF), BF16),
            pltpu.VMEM((HALF, ROWS), BF16),
            pltpu.VMEM(slots, BF16),
            pltpu.VMEM(slots, BF16),
            pltpu.VMEM(slots, BF16),
            pltpu.VMEM(slots, BF16),
            pltpu.VMEM(logs, F32),
            pltpu.VMEM(logs, F32),
            pltpu.VMEM((STEPS, HL, REQ, HD), F32),
            pltpu.VMEM((STEPS, HL, REQ, HD), F32),
            pltpu.VMEM((HL, REQ, HD), F32),
            pltpu.VMEM((STEPS, REQ, HL * HD), BF16),
            pltpu.VMEM((NY, 2, REQ, SHARE), F32),
            pltpu.VMEM((STEPS, NY, REQ, SHARE), F32),
            pltpu.VMEM((STEPS, NY, REQ, SHARE), BF16),
            pltpu.VMEM((STEPS, NY, REQ, SHARE), BF16),
            pltpu.VMEM((STEPS, NY - 1, REQ, SHARE), BF16),
            dma((STEPS + 6 + 2 * NY,)),
            dma((STEPS,)),
        ] + [dma((STEPS,))] * 2 + [dma((STEPS + 1,))] * 2 + [dma((STEPS,))] * 2 + [dma((STEPS, NY))] * 2 + [dma((STEPS,))] * 2,
        compiler_params=pltpu.CompilerParams(
            collective_id=0, has_side_effects=True, vmem_limit_bytes=62 * 2**20
        ),
        name="attention",
    )(
        queries, prefix_of.reshape(1, REQ), suffix_len.reshape(1, REQ), new_keys, new_values,
        suffix_keys, suffix_values, prefix_keys, prefix_values, out_weight,
    )
    for dy in range(NY - 1):
        own = own + parts[:, dy].astype(F32)
    return own.astype(BF16)


def solution(mesh):
    return jax.shard_map(
        body,
        mesh=mesh,
        in_specs=(
            P(None, "wide", "tensor"),
            P(None, "wide", "tensor"),
            P(None, "wide", "tensor"),
            P("wide", None, "tensor"),
            P("wide", None, "tensor"),
            P("wide"),
            P("wide", None, "tensor"),
            P("wide", None, "tensor"),
            P("wide", None),
            P("tensor", None),
        ),
        out_specs=P(None, "wide", "tensor"),
        check_vma=False,
    )
```

```python
import functools

import jax
import jax.numpy as jnp
from jax import lax
from jax.experimental import pallas as pl
from jax.experimental.pallas import tpu as pltpu
from jax.sharding import PartitionSpec as P

MESH = pl.DeviceIdType.MESH
HD = 128
NZ, NX, NY = 8, 4, 4
NW = NZ * NX
STEPS, REQ, HL = 4, 64, 8
PRE, SUF = 768, 64
ROWS = HL * REQ
HALF = ROWS // 2
LAST = STEPS - 1
EARLY = 2
FIRST = 1
SCALE = HD ** (-0.5)
LOG2E = 1.4426950408889634
BLOCK = 8
LKEYS = BLOCK * SUF
DOUT = 4096
SHARE = 512
F32, BF16, I32 = jnp.float32, jnp.bfloat16, jnp.int32


def is_early(s):
    return FIRST <= s < FIRST + EARLY


def dot(a, b):
    return lax.dot_general(a, b, (((1,), (0,)), ((), ())), preferred_element_type=F32)


def dot_t(a, b):
    return lax.dot_general(a, b, (((1,), (1,)), ((), ())), preferred_element_type=F32)


def kernel(
    q_hbm, pof_ref, len_ref, nk_hbm, nv_hbm, sk_hbm, sv_hbm, pk_hbm, pv_hbm, w_hbm,
    own_hbm, y_recv,
    q, nk, nv, sk, sv, pk, pv, w, vones, qf, nkf, nvf, kloc, vloc,
    len_col,
    spread, gather, q_send, q_recv, r_send, r_recv, l_send, l_recv,
    loc_out, loc_log, pre_part, attn, early, kept, given, c_recv, y_send,
    order_in, order_out, pick_out, f_send, f_recv, raw, slot_attn, kept_e, given_e, c_recv_e,
    y_send_e, y_recv_e, p_send, p_recv, own_v,
    in_sems, out_sems, qs, qr, rs, rr, ls, lr, cs, cr, ys, yr, fs, fr, cse, cre, yse, yre, ps, pr,
):
    me_w, me_t = lax.axis_index("wide"), lax.axis_index("tensor")
    z, x = me_w // NX, me_w % NX
    y, c = me_t // 2, me_t % 2

    def offset(i):
        zi = i // NX
        half = (zi + 1) // 2
        dz = lax.rem(jnp.where(lax.rem(zi, 2) == 1, half, NZ - half), NZ)
        return dz, lax.rem(i, NX)

    def ahead(dz, dx):
        return (lax.rem(z + dz, NZ) * NX + lax.rem(x + dx, NX), me_t)

    def behind(dz, dx):
        return (lax.rem(z + NZ - dz, NZ) * NX + lax.rem(x + NX - dx, NX), me_t)

    def across(dy):
        return (me_w, lax.rem(y + dy, NY) * 2 + c)

    other = (me_w, y * 2 + 1 - c)

    loads = [
        pltpu.make_async_copy(src, dst, in_sems.at[n])
        for n, (src, dst) in enumerate(
            [(q_hbm.at[s], q.at[s]) for s in range(STEPS)]
            + [(pk_hbm, pk), (pv_hbm, pv), (nk_hbm, nk), (nv_hbm, nv), (sk_hbm, sk), (sv_hbm, sv)]
            + [(w_hbm.at[:, pl.ds(n * SHARE, SHARE)], w.at[n]) for n in range(2 * NY)]
        )
    ]
    for load in loads[:STEPS]:
        load.start()

    barrier = pltpu.get_barrier_semaphore()

    def greet(i, carry):
        pl.semaphore_signal(barrier, inc=1, device_id=ahead(*offset(i)), device_id_type=MESH)
        return carry

    lax.fori_loop(1, NW, greet, 0)
    for dy in range(1, NY):
        pl.semaphore_signal(barrier, inc=1, device_id=across(dy), device_id_type=MESH)
    pl.semaphore_signal(barrier, inc=1, device_id=other, device_id_type=MESH)

    pof = pof_ref[...]
    sub = lax.broadcasted_iota(I32, (REQ, REQ), 0)
    lane = lax.broadcasted_iota(I32, (REQ, REQ), 1)

    def upright(row):
        return jnp.sum(jnp.where(sub == lane, row, 0), axis=1, keepdims=True)

    rank = jnp.sum(
        jnp.where((upright(pof) == pof) & (sub < lane), 1, 0), axis=0, keepdims=True
    )
    owner = lax.shift_right_logical(pof, 1)
    dz = lax.bitwise_and(lax.shift_right_logical(owner, 2) - z + NZ, NZ - 1)
    dx = lax.bitwise_and(lax.bitwise_and(owner, NX - 1) - x + NX, NX - 1)
    slot = (dz * NX + dx) * 16 + lax.bitwise_and(pof, 1) * 8 + rank
    slot_col = upright(slot)
    wide_sub = lax.broadcasted_iota(I32, (REQ, HALF), 0)
    wide_lane = lax.broadcasted_iota(I32, (REQ, HALF), 1)
    key_row = jnp.sum(
        jnp.where(wide_sub == lax.bitwise_and(wide_lane, REQ - 1), slot_col, 0),
        axis=0, keepdims=True,
    ) + 2 * lax.shift_right_logical(lax.broadcasted_iota(I32, (1, HALF), 1), 6)
    hit = lax.broadcasted_iota(I32, (ROWS, HALF), 0) == key_row
    spread[...] = jnp.where(hit, 1.0, 0.0).astype(BF16)

    def dispatch(s):
        if s < 2:
            loads[s].wait()
        for half in range(2):
            stacked = jnp.concatenate(
                [q[s, :, h * HD:(h + 1) * HD] for h in range(half * 4, half * 4 + 4)], axis=0
            )
            placed = dot(spread[...], stacked).astype(BF16).reshape(NW, 16, HD)
            q_send[s, :, half] = placed
            q_recv[s, 0, half] = placed[0]

    def send_queries(s):
        def one(i, carry):
            dz, dx = offset(NW - i)
            o = dz * NX + dx
            pltpu.make_async_remote_copy(
                src_ref=q_send.at[s, o], dst_ref=q_recv.at[s, o], send_sem=qs.at[s],
                recv_sem=qr.at[s], device_id=ahead(dz, dx), device_id_type=MESH,
            ).start()
            return carry

        lax.fori_loop(1, NW, one, 0)

    def send_results(s, half=None):
        part = pl.ds(0, 2) if half is None else pl.ds(half, 1)

        def one(i, carry):
            dz, dx = offset(NW - i)
            o = dz * NX + dx
            pltpu.make_async_remote_copy(
                src_ref=r_send.at[s, o, part], dst_ref=r_recv.at[s, o, part],
                send_sem=rs.at[s + (half or 0)], recv_sem=rr.at[s + (half or 0)],
                device_id=behind(dz, dx), device_id_type=MESH,
            ).start()
            return carry

        lax.fori_loop(1, NW, one, 0)

    def send_early_logs():
        def one(i, carry):
            dz, dx = offset(NW - i)
            o = dz * NX + dx
            pltpu.make_async_remote_copy(
                src_ref=f_send.at[o], dst_ref=f_recv.at[o], send_sem=fs,
                recv_sem=fr, device_id=ahead(dz, dx), device_id_type=MESH,
            ).start()
            return carry

        lax.fori_loop(1, NW, one, 0)

    def send_projected(s):
        def one(i, carry):
            dz, dx = offset(NW - i)
            o = dz * NX + dx
            pltpu.make_async_remote_copy(
                src_ref=p_send.at[s, o], dst_ref=p_recv.at[s, o], send_sem=ps.at[s],
                recv_sem=pr.at[s], device_id=behind(dz, dx), device_id_type=MESH,
            ).start()
            return carry

        lax.fori_loop(1, NW, one, 0)

    def send_logs(s):
        def one(i, carry):
            dz, dx = offset(NW - i)
            o = dz * NX + dx
            pltpu.make_async_remote_copy(
                src_ref=l_send.at[s, o], dst_ref=l_recv.at[s, o], send_sem=ls.at[s],
                recv_sem=lr.at[s], device_id=behind(dz, dx), device_id_type=MESH,
            ).start()
            return carry

        lax.fori_loop(1, NW, one, 0)

    def await_all(ref, sem):
        pltpu.make_async_copy(ref, ref, sem).wait()

    dispatch(0)
    pl.semaphore_wait(barrier, NW - 1 + NY - 1 + 1)
    send_queries(0)
    for load in loads[STEPS:]:
        load.start()
    dispatch(1)
    send_queries(1)

    len_col[...] = jnp.broadcast_to(upright(len_ref[...]), (REQ, HD))
    for load in loads[6:10]:
        load.wait()
    loads[2].wait()
    loads[3].wait()
    qf[...] = q[...].astype(F32)
    nkf[...] = nk[...].astype(F32)
    nvf[...] = nv[...].astype(F32)
    kloc[LKEYS:] = jnp.zeros((HD, HD), BF16)
    vloc[LKEYS:, :HD] = jnp.zeros((HD, HD), BF16)
    vloc[:, HD:] = jnp.ones((LKEYS + HD, HD), BF16)
    own_i = lax.broadcasted_iota(I32, (BLOCK, LKEYS), 0)
    own_k = lax.broadcasted_iota(I32, (BLOCK, LKEYS), 1)
    own_hit = lax.shift_right_logical(own_k, 6) == own_i
    own_j = lax.bitwise_and(own_k, SUF - 1)
    new_s = lax.broadcasted_iota(I32, (STEPS, BLOCK, HD), 0)
    new_i = lax.broadcasted_iota(I32, (STEPS, BLOCK, HD), 1)
    new_k = lax.broadcasted_iota(I32, (STEPS, BLOCK, HD), 2)
    new_hit = (lax.bitwise_and(new_k, BLOCK - 1) == new_i) & (
        lax.shift_right_logical(new_k, 3) <= new_s
    )

    def local_block(b, carry):
        rows = pl.ds(pl.multiple_of(b * BLOCK, BLOCK), BLOCK)
        query = jnp.concatenate(
            [qf[s, rows, h * HD:(h + 1) * HD] for s in range(STEPS) for h in range(HL)], axis=0
        ).astype(BF16)
        kloc[:LKEYS] = sk[rows].reshape(LKEYS, HD)
        vloc[:LKEYS, :HD] = sv[rows].reshape(LKEYS, HD)
        kloc[LKEYS:LKEYS + STEPS * BLOCK] = nkf[:, rows, :].reshape(STEPS * BLOCK, HD).astype(BF16)
        vloc[LKEYS:LKEYS + STEPS * BLOCK, :HD] = (
            nvf[:, rows, :].reshape(STEPS * BLOCK, HD).astype(BF16)
        )
        length = len_col[rows, :1]
        past = dot_t(query, kloc[:LKEYS]).reshape(STEPS * HL, BLOCK, LKEYS)
        past = jnp.where((own_hit & (own_j < length))[None], past, -jnp.inf)
        fresh = dot_t(query, kloc[LKEYS:]).reshape(STEPS, HL, BLOCK, HD)
        fresh = jnp.where(new_hit[:, None], fresh, -jnp.inf)
        past = past.reshape(STEPS * HL * BLOCK, LKEYS)
        fresh = fresh.reshape(STEPS * HL * BLOCK, HD)
        top = jnp.maximum(
            jnp.max(past, axis=-1, keepdims=True), jnp.max(fresh, axis=-1, keepdims=True)
        )
        past = jnp.exp2((past - top) * (SCALE * LOG2E)).astype(BF16)
        fresh = jnp.exp2((fresh - top) * (SCALE * LOG2E)).astype(BF16)
        both = dot(past, vloc[:LKEYS]) + dot(fresh, vloc[LKEYS:])
        total = both[:, HD:]
        shape = (STEPS, HL, BLOCK, HD)
        loc_out[:, :, rows, :] = (both[:, :HD] / total).reshape(shape)
        loc_log[:, :, rows, :] = (top * SCALE + jnp.log(total)).reshape(shape)
        return carry

    lax.fori_loop(0, REQ // BLOCK, local_block, 0)

    own = jnp.broadcast_to(lax.shift_right_logical(slot_col, 4), (REQ, HD))
    pick = lax.bitwise_and(slot_col, 8) * 2 + lax.bitwise_and(slot_col, 1)
    lanes = lax.broadcasted_iota(I32, (REQ, HD), 1)

    logs_out = jnp.zeros((REQ, HD), F32)
    for e in range(EARLY):
        for h in range(HL):
            logs_out = jnp.where(lanes == pick + (e * 32 + 2 * h), loc_log[FIRST + e, h], logs_out)
    for o in range(NW):
        row = jnp.sum(jnp.where(own == o, logs_out, 0.0), axis=0, keepdims=True)
        f_send[o] = row
        if o == 0:
            f_recv[o] = row
    send_early_logs()
    dispatch(2)
    send_queries(2)
    dispatch(3)
    send_queries(3)

    tall_sub = lax.broadcasted_iota(I32, (HALF, REQ), 0)
    tall_lane = lax.broadcasted_iota(I32, (HALF, REQ), 1)
    key_col = jnp.sum(
        jnp.where(lax.bitwise_and(tall_sub, REQ - 1) == tall_lane, slot, 0),
        axis=1, keepdims=True,
    ) + 2 * lax.shift_right_logical(lax.broadcasted_iota(I32, (HALF, 1), 0), 6)
    hit = lax.broadcasted_iota(I32, (HALF, ROWS), 1) == key_col
    gather[...] = jnp.where(hit, 1.0, 0.0).astype(BF16)
    slot_out = (
        lax.shift_left(lax.shift_right_logical(slot, 4), 4)
        + lax.shift_right_logical(lax.bitwise_and(slot, 8), 2) + lax.bitwise_and(slot, 1)
    )
    key_out = jnp.sum(
        jnp.where(lax.bitwise_and(tall_sub, REQ - 1) == tall_lane, slot_out, 0),
        axis=1, keepdims=True,
    ) + 4 * lax.shift_right_logical(lax.broadcasted_iota(I32, (HALF, 1), 0), 6)
    hit = lax.broadcasted_iota(I32, (HALF, ROWS), 1) == key_out
    pick_out[...] = jnp.where(hit, 1.0, 0.0).astype(BF16)
    at = lax.broadcasted_iota(I32, (ROWS, 1), 0)
    column = lax.broadcasted_iota(I32, (ROWS, ROWS), 1)
    turn = lax.bitwise_and(at, 1)
    target = (
        lax.bitwise_and(lax.shift_right_logical(at, 1), NW - 1) * 16
        + lax.shift_right_logical(at, 6) * 2 + turn
    )
    order_in[...] = jnp.where(column == target, 1.0, 0.0).astype(BF16)
    target = (
        lax.bitwise_and(lax.shift_right_logical(at, 2), 3) * 128
        + lax.bitwise_and(lax.shift_right_logical(at, 1), 1) * 64
        + lax.shift_right_logical(at, 4) * 2 + turn
    )
    order_out[...] = jnp.where(column == target, 1.0, 0.0).astype(BF16)
    loads[4].wait()
    loads[5].wait()
    vones[:, :, :HD] = pv[...]
    vones[:, :, HD:] = jnp.ones((2, PRE, HD), BF16)


    log_lane = lax.broadcasted_iota(I32, (1, 2 * HL, HD), 2)
    place = lax.broadcasted_iota(I32, (1, 2 * HL, HD), 1)
    PART = 16

    def attend(s):
        await_all(q_recv.at[s, pl.ds(1, NW - 1)], qr.at[s])

        def part(i, carry):
            some = pl.ds(i * PART, PART)
            logs = jnp.zeros((PART, 2 * HL, HD), F32)
            arrived = q_recv[s, some].astype(F32)
            results = []
            for p in range(2):
                rows = slice(p * 8, p * 8 + 8)
                query = jnp.concatenate([arrived[:, 0, rows], arrived[:, 1, rows]], axis=1)
                scores = dot_t(query.astype(BF16).reshape(PART * 2 * HL, HD), pk[p])
                top = jnp.max(scores, axis=-1, keepdims=True)
                weights = jnp.exp2((scores - top) * (SCALE * LOG2E)).astype(BF16)
                both = dot(weights, vones[p])
                total = both[:, HD:]
                result = (both[:, :HD] / total).reshape(PART, 2 * HL, HD)
                log = (top * SCALE + jnp.log(total)).reshape(PART, 2 * HL, HD)
                if is_early(s):
                    there = jnp.where(
                        log_lane == place + ((s - FIRST) * 32 + p * 2 * HL), f_recv[some], 0.0
                    )
                    there = jnp.sum(there, axis=-1, keepdims=True)
                    high = jnp.maximum(log, there)
                    a, b = jnp.exp(log - high), jnp.exp(there - high)
                    raw[p, some] = (result * (a / (a + b))).astype(BF16)
                results.append(result)
                logs = jnp.where(log_lane == place + p * 2 * HL, log, logs)
            for half in range(0 if is_early(s) else 2):
                rows = slice(half * 8, half * 8 + 8)
                r_send[s, some, half] = jnp.concatenate(
                    [results[0][:, rows], results[1][:, rows]], axis=1
                ).astype(BF16)
            l_send[s, some] = jnp.sum(logs, axis=1, keepdims=True)
            return carry

        lax.fori_loop(0, NW // PART, part, 0)
        l_recv[s, 0] = l_send[s, 0]
        send_logs(s)
        if is_early(s):
            for p in range(2):
                moved = dot(order_in[...], raw[p].reshape(ROWS, HD)).astype(BF16)
                for h in range(HL):
                    slot_attn[p, :, h * HD:(h + 1) * HD] = moved[h * REQ:(h + 1) * REQ]
            return
        r_recv[s, 0] = r_send[s, 0]
        if s == LAST:
            send_results(s, 0)
            send_results(s, 1)
        else:
            send_results(s)

    def merge(s):
        await_all(l_recv.at[s, pl.ds(1, NW - 1)], lr.at[s])
        logs = jnp.zeros((REQ, HD), F32)
        for o in range(NW):
            logs = jnp.where(own == o, l_recv[s, o], logs)
        for h in range(HL):
            pre = jnp.sum(jnp.where(lanes == pick + 2 * h, logs, 0.0), axis=1, keepdims=True)
            loc = loc_log[s, h]
            high = jnp.maximum(pre, loc)
            a, b = jnp.exp(pre - high), jnp.exp(loc - high)
            mine = loc_out[s, h] * (b / (a + b))
            if is_early(s):
                attn[s, :, h * HD:(h + 1) * HD] = mine.astype(BF16)
            else:
                pre_part[h] = a / (a + b)
                loc_out[s, h] = mine

    def take(s, half):
        back = dot(gather[...], r_recv[s, :, half].reshape(ROWS, HD))
        for n in range(4):
            h = half * 4 + n
            joint = pre_part[h] * back[n * REQ:(n + 1) * REQ] + loc_out[s, h]
            attn[s, :, h * HD:(h + 1) * HD] = joint.astype(BF16)

    def block(dy, core):
        return lax.rem(y + dy, NY) * 2 + core

    WIDE = HL * HD // 2

    def term(s, dy, side):
        n = block(dy, 1 - c if side else c)
        if s == LAST:
            return early[dy, side] + dot(attn[s, :, WIDE:], w[n, WIDE:])
        return dot(attn[s], w[n])

    def begin(s):
        for side in (1, 0):
            for dy in (2, 1, 3, 0):
                n = block(dy, 1 - c if side else c)
                early[dy, side] = dot(attn[s, :, :WIDE], w[n, :WIDE])

    def give(s, dy):
        given[s, dy] = term(s, dy, 1).astype(BF16)
        pltpu.make_async_remote_copy(
            src_ref=given.at[s, dy], dst_ref=c_recv.at[s, dy], send_sem=cs.at[s, dy],
            recv_sem=cr.at[s, dy], device_id=other, device_id_type=MESH,
        ).start()

    def keep(s, dy):
        kept[s, dy] = term(s, dy, 0)

    def pair(s, dy):
        await_all(c_recv.at[s, dy], cr.at[s, dy])
        both = kept[s, dy] + c_recv[s, dy].astype(F32)
        if dy == 0:
            kept[s, dy] = both
            pltpu.make_async_copy(kept.at[s, dy], own_hbm.at[s], out_sems.at[s]).start()
            return
        y_send[s, dy - 1] = both.astype(BF16)
        pltpu.make_async_remote_copy(
            src_ref=y_send.at[s, dy - 1], dst_ref=y_recv.at[dy - 1, s],
            send_sem=ys.at[s], recv_sem=yr.at[s], device_id=across(dy), device_id_type=MESH,
        ).start()

    def project(s):
        give(s, 2)
        give(s, 1)
        give(s, 3)
        keep(s, 2)
        keep(s, 1)
        pair(s, 2)
        keep(s, 3)
        pair(s, 1)
        give(s, 0)
        pair(s, 3)
        keep(s, 0)
        pair(s, 0)

    def rows_of(u):
        if u < EARLY:
            return slot_attn[...].reshape(2 * REQ, HL * HD)
        return attn[FIRST:FIRST + EARLY].reshape(2 * REQ, HL * HD)

    def give_early(u, dy):
        term = dot(rows_of(u), w[block(dy, 1 - c)]).astype(BF16)
        given_e[u, dy] = term.reshape(2, REQ, SHARE)
        pltpu.make_async_remote_copy(
            src_ref=given_e.at[u, dy], dst_ref=c_recv_e.at[u, dy], send_sem=cse.at[u, dy],
            recv_sem=cre.at[u, dy], device_id=other, device_id_type=MESH,
        ).start()

    def keep_early(u, dy):
        kept_e[u, dy] = dot(rows_of(u), w[block(dy, c)]).reshape(2, REQ, SHARE)

    def pair_early(u, dy):
        await_all(c_recv_e.at[u, dy], cre.at[u, dy])
        both = kept_e[u, dy] + c_recv_e[u, dy].astype(F32)
        if dy == 0:
            kept_e[u, dy] = both
            return
        y_send_e[u, dy - 1] = both.astype(BF16)
        target = y_recv_e.at[u, dy - 1] if u < EARLY else y_recv.at[dy - 1, pl.ds(FIRST, EARLY)]
        pltpu.make_async_remote_copy(
            src_ref=y_send_e.at[u, dy - 1], dst_ref=target, send_sem=yse.at[u],
            recv_sem=yre.at[u], device_id=across(dy), device_id_type=MESH,
        ).start()

    def project_early(u):
        give_early(u, 2)
        give_early(u, 1)
        give_early(u, 3)
        keep_early(u, 2)
        keep_early(u, 1)
        pair_early(u, 2)
        keep_early(u, 3)
        pair_early(u, 1)
        give_early(u, 0)
        pair_early(u, 3)
        keep_early(u, 0)
        pair_early(u, 0)

    def return_early(s):
        await_all(y_recv_e.at[s], yre.at[s])
        total = kept_e[s, 0]
        for dy in range(NY - 1):
            total = total + y_recv_e[s, dy].astype(F32)
        total = total.astype(BF16).reshape(2 * REQ, SHARE)
        stacked = jnp.concatenate([total[:, j * HD:(j + 1) * HD] for j in range(4)], axis=0)
        placed = dot(order_out[...], stacked).astype(BF16).reshape(NW, 16, HD)
        p_send[s] = placed
        p_recv[s, 0] = placed[0]
        send_projected(s)

    def combine_early(s):
        await_all(p_recv.at[s, pl.ds(1, NW - 1)], pr.at[s])
        back = dot(pick_out[...], p_recv[s].reshape(ROWS, HD))
        for j in range(4):
            cols = slice(j * HD, (j + 1) * HD)
            own_v[s, :, cols] = kept_e[EARLY, 0, s, :, cols] + back[j * REQ:(j + 1) * REQ]
        pltpu.make_async_copy(own_v.at[s], own_hbm.at[FIRST + s], out_sems.at[FIRST + s]).start()

    def step(s):
        merge(s)
        if s == LAST:
            for half in range(2):
                await_all(r_recv.at[s, pl.ds(1, NW - 1), half], rr.at[s + half])
                take(s, half)
                if half == 0:
                    begin(s)
        else:
            await_all(r_recv.at[s, pl.ds(1, NW - 1)], rr.at[s])
            take(s, 0)
            take(s, 1)
        project(s)

    attend(0)
    await_all(f_recv.at[pl.ds(1, NW - 1)], fr)
    attend(1)
    for load in loads[10:]:
        load.wait()
    project_early(0)
    attend(2)
    project_early(1)
    return_early(0)
    attend(3)
    merge(1)
    merge(2)
    project_early(2)
    step(0)
    return_early(1)
    combine_early(0)
    step(3)
    combine_early(1)

    await_all(f_send.at[pl.ds(1, NW - 1)], fs)
    for u in range(EARLY + 1):
        for dy in range(NY):
            await_all(given_e.at[u, dy], cse.at[u, dy])
        await_all(y_send_e.at[u], yse.at[u])
    await_all(y_recv.at[:, pl.ds(FIRST, EARLY)], yre.at[EARLY])
    for s in range(EARLY):
        await_all(p_send.at[s, pl.ds(1, NW - 1)], ps.at[s])
        pltpu.make_async_copy(own_v.at[s], own_hbm.at[FIRST + s], out_sems.at[FIRST + s]).wait()
    for s in range(STEPS):
        await_all(q_send.at[s, pl.ds(1, NW - 1)], qs.at[s])
        await_all(l_send.at[s, pl.ds(1, NW - 1)], ls.at[s])
        if is_early(s):
            continue
        if s == LAST:
            for half in range(2):
                await_all(r_send.at[s, pl.ds(1, NW - 1), half], rs.at[s + half])
        else:
            await_all(r_send.at[s, pl.ds(1, NW - 1)], rs.at[s])
        for dy in range(NY):
            await_all(given.at[s, dy], cs.at[s, dy])
        await_all(y_send.at[s], ys.at[s])
        pltpu.make_async_copy(kept.at[s, 0], own_hbm.at[s], out_sems.at[s]).wait()
    for s in range(STEPS):
        if not is_early(s):
            await_all(y_recv.at[:, s], yr.at[s])


def body(
    queries, new_keys, new_values, suffix_keys, suffix_values, suffix_len,
    prefix_keys, prefix_values, prefix_of, out_weight,
):
    anywhere = pl.BlockSpec(memory_space=pl.ANY)
    vmem = pl.BlockSpec(memory_space=pltpu.VMEM)
    dma = pltpu.SemaphoreType.DMA
    slots = (STEPS, NW, 2, 16, HD)
    logs = (STEPS, NW, 1, HD)
    own, parts = pl.pallas_call(
        kernel,
        out_shape=(
            jax.ShapeDtypeStruct((STEPS, REQ, SHARE), F32),
            jax.ShapeDtypeStruct((NY - 1, STEPS, REQ, SHARE), BF16),
        ),
        in_specs=[anywhere, vmem, vmem] + [anywhere] * 7,
        out_specs=(anywhere, anywhere),
        scratch_shapes=[
            pltpu.VMEM(queries.shape, BF16),
            pltpu.VMEM(new_keys.shape, BF16),
            pltpu.VMEM(new_values.shape, BF16),
            pltpu.VMEM(suffix_keys.shape, BF16),
            pltpu.VMEM(suffix_values.shape, BF16),
            pltpu.VMEM(prefix_keys.shape, BF16),
            pltpu.VMEM(prefix_values.shape, BF16),
            pltpu.VMEM((2 * NY, out_weight.shape[0], SHARE), BF16),
            pltpu.VMEM((2, PRE, 2 * HD), BF16),
            pltpu.VMEM(queries.shape, F32),
            pltpu.VMEM(new_keys.shape, F32),
            pltpu.VMEM(new_values.shape, F32),
            pltpu.VMEM((LKEYS + HD, HD), BF16),
            pltpu.VMEM((LKEYS + HD, 2 * HD), BF16),
            pltpu.VMEM((REQ, HD), I32),
            pltpu.VMEM((ROWS, HALF), BF16),
            pltpu.VMEM((HALF, ROWS), BF16),
            pltpu.VMEM(slots, BF16),
            pltpu.VMEM(slots, BF16),
            pltpu.VMEM(slots, BF16),
            pltpu.VMEM(slots, BF16),
            pltpu.VMEM(logs, F32),
            pltpu.VMEM(logs, F32),
            pltpu.VMEM((STEPS, HL, REQ, HD), F32),
            pltpu.VMEM((STEPS, HL, REQ, HD), F32),
            pltpu.VMEM((HL, REQ, HD), F32),
            pltpu.VMEM((STEPS, REQ, HL * HD), BF16),
            pltpu.VMEM((NY, 2, REQ, SHARE), F32),
            pltpu.VMEM((STEPS, NY, REQ, SHARE), F32),
            pltpu.VMEM((STEPS, NY, REQ, SHARE), BF16),
            pltpu.VMEM((STEPS, NY, REQ, SHARE), BF16),
            pltpu.VMEM((STEPS, NY - 1, REQ, SHARE), BF16),
            pltpu.VMEM((ROWS, ROWS), BF16),
            pltpu.VMEM((ROWS, ROWS), BF16),
            pltpu.VMEM((HALF, ROWS), BF16),
            pltpu.VMEM((NW, 1, HD), F32),
            pltpu.VMEM((NW, 1, HD), F32),
            pltpu.VMEM((2, NW, 16, HD), BF16),
            pltpu.VMEM((2, REQ, HL * HD), BF16),
            pltpu.VMEM((EARLY + 1, NY, 2, REQ, SHARE), F32),
            pltpu.VMEM((EARLY + 1, NY, 2, REQ, SHARE), BF16),
            pltpu.VMEM((EARLY + 1, NY, 2, REQ, SHARE), BF16),
            pltpu.VMEM((EARLY + 1, NY - 1, 2, REQ, SHARE), BF16),
            pltpu.VMEM((EARLY, NY - 1, 2, REQ, SHARE), BF16),
            pltpu.VMEM((EARLY, NW, 16, HD), BF16),
            pltpu.VMEM((EARLY, NW, 16, HD), BF16),
            pltpu.VMEM((EARLY, REQ, SHARE), F32),
            dma((STEPS + 6 + 2 * NY,)),
            dma((STEPS,)),
        ] + [dma((STEPS,))] * 2 + [dma((STEPS + 1,))] * 2 + [dma((STEPS,))] * 2 + [dma((STEPS, NY))] * 2 + [dma((STEPS,))] * 2
        + [dma, dma] + [dma((EARLY + 1, NY))] * 2 + [dma((EARLY + 1,))] * 2 + [dma((EARLY,))] * 2,
        compiler_params=pltpu.CompilerParams(
            collective_id=0, has_side_effects=True, vmem_limit_bytes=62 * 2**20
        ),
        name="attention",
    )(
        queries, prefix_of.reshape(1, REQ), suffix_len.reshape(1, REQ), new_keys, new_values,
        suffix_keys, suffix_values, prefix_keys, prefix_values, out_weight,
    )
    for dy in range(NY - 1):
        own = own + parts[dy].astype(F32)
    return own.astype(BF16)


def solution(mesh):
    return jax.shard_map(
        body,
        mesh=mesh,
        in_specs=(
            P(None, "wide", "tensor"),
            P(None, "wide", "tensor"),
            P(None, "wide", "tensor"),
            P("wide", None, "tensor"),
            P("wide", None, "tensor"),
            P("wide"),
            P("wide", None, "tensor"),
            P("wide", None, "tensor"),
            P("wide", None),
            P("tensor", None),
        ),
        out_specs=P(None, "wide", "tensor"),
        check_vma=False,
    )
```

```python
import functools

import jax
import jax.numpy as jnp
from jax import lax
from jax.experimental import pallas as pl
from jax.experimental.pallas import tpu as pltpu
from jax.sharding import PartitionSpec as P

MESH = pl.DeviceIdType.MESH
HD = 128
NZ, NX, NY = 8, 4, 4
NW = NZ * NX
STEPS, REQ, HL = 4, 64, 8
PRE, SUF = 768, 64
ROWS = HL * REQ
HALF = ROWS // 2
LAST = STEPS - 1
EARLY = 2
FIRST = 1
SCALE = HD ** (-0.5)
LOG2E = 1.4426950408889634
BLOCK = 8
LKEYS = BLOCK * SUF
DOUT = 4096
SHARE = 512
F32, BF16, I32 = jnp.float32, jnp.bfloat16, jnp.int32


def is_early(s):
    return FIRST <= s < FIRST + EARLY


def dot(a, b):
    return lax.dot_general(a, b, (((1,), (0,)), ((), ())), preferred_element_type=F32)


def dot_t(a, b):
    return lax.dot_general(a, b, (((1,), (1,)), ((), ())), preferred_element_type=F32)


def kernel(
    q_hbm, pof_hbm, len_hbm, nk_hbm, nv_hbm, sk_hbm, sv_hbm, pk_hbm, pv_hbm, w_hbm,
    own_hbm, y_recv,
    q, nk, nv, sk, sv, pk, pv, w, vones, qf, nkf, nvf, kloc, vloc,
    pof_ref, len_ref, len_col,
    spread, gather, q_send, q_recv, r_send, r_recv, l_send, l_recv,
    loc_out, loc_log, pre_part, attn, early, kept, given, c_recv, y_send,
    order_in, order_out, pick_out, f_send, f_recv, raw, slot_attn, kept_e, given_e, c_recv_e,
    y_send_e, y_recv_e, p_send, p_recv, own_v,
    in_sems, out_sems, qs, qr, rs, rr, ls, lr, cs, cr, ys, yr, fs, fr, cse, cre, yse, yre, ps, pr,
):
    me_w, me_t = lax.axis_index("wide"), lax.axis_index("tensor")
    z, x = me_w // NX, me_w % NX
    y, c = me_t // 2, me_t % 2

    def offset(i):
        zi = i // NX
        half = (zi + 1) // 2
        dz = lax.rem(jnp.where(lax.rem(zi, 2) == 1, half, NZ - half), NZ)
        return dz, lax.rem(i, NX)

    def ahead(dz, dx):
        return (lax.rem(z + dz, NZ) * NX + lax.rem(x + dx, NX), me_t)

    def behind(dz, dx):
        return (lax.rem(z + NZ - dz, NZ) * NX + lax.rem(x + NX - dx, NX), me_t)

    def across(dy):
        return (me_w, lax.rem(y + dy, NY) * 2 + c)

    other = (me_w, y * 2 + 1 - c)

    loads = [
        pltpu.make_async_copy(src, dst, in_sems.at[n])
        for n, (src, dst) in enumerate(
            [(q_hbm.at[s], q.at[s]) for s in range(STEPS)]
            + [(pk_hbm, pk), (pv_hbm, pv), (nk_hbm, nk), (nv_hbm, nv), (sk_hbm, sk), (sv_hbm, sv)]
            + [(w_hbm.at[:, pl.ds(n * SHARE, SHARE)], w.at[n]) for n in range(2 * NY)]
        )
    ]
    tables = [
        pltpu.make_async_copy(src, dst, in_sems.at[len(loads) + n])
        for n, (src, dst) in enumerate([(pof_hbm, pof_ref), (len_hbm, len_ref)])
    ]
    for load in tables + loads[:STEPS]:
        load.start()

    barrier = pltpu.get_barrier_semaphore()

    def greet(i, carry):
        pl.semaphore_signal(barrier, inc=1, device_id=ahead(*offset(i)), device_id_type=MESH)
        return carry

    lax.fori_loop(1, NW, greet, 0)
    for dy in range(1, NY):
        pl.semaphore_signal(barrier, inc=1, device_id=across(dy), device_id_type=MESH)
    pl.semaphore_signal(barrier, inc=1, device_id=other, device_id_type=MESH)

    tables[0].wait()
    pof = pof_ref[...]
    sub = lax.broadcasted_iota(I32, (REQ, REQ), 0)
    lane = lax.broadcasted_iota(I32, (REQ, REQ), 1)

    def upright(row):
        return jnp.sum(jnp.where(sub == lane, row, 0), axis=1, keepdims=True)

    rank = jnp.sum(
        jnp.where((upright(pof) == pof) & (sub < lane), 1, 0), axis=0, keepdims=True
    )
    owner = lax.shift_right_logical(pof, 1)
    dz = lax.bitwise_and(lax.shift_right_logical(owner, 2) - z + NZ, NZ - 1)
    dx = lax.bitwise_and(lax.bitwise_and(owner, NX - 1) - x + NX, NX - 1)
    slot = (dz * NX + dx) * 16 + lax.bitwise_and(pof, 1) * 8 + rank
    slot_col = upright(slot)
    wide_sub = lax.broadcasted_iota(I32, (REQ, HALF), 0)
    wide_lane = lax.broadcasted_iota(I32, (REQ, HALF), 1)
    key_row = jnp.sum(
        jnp.where(wide_sub == lax.bitwise_and(wide_lane, REQ - 1), slot_col, 0),
        axis=0, keepdims=True,
    ) + 2 * lax.shift_right_logical(lax.broadcasted_iota(I32, (1, HALF), 1), 6)
    hit = lax.broadcasted_iota(I32, (ROWS, HALF), 0) == key_row
    spread[...] = jnp.where(hit, 1.0, 0.0).astype(BF16)

    def dispatch(s):
        if s < 2:
            loads[s].wait()
        for half in range(2):
            stacked = jnp.concatenate(
                [q[s, :, h * HD:(h + 1) * HD] for h in range(half * 4, half * 4 + 4)], axis=0
            )
            placed = dot(spread[...], stacked).astype(BF16).reshape(NW, 16, HD)
            q_send[s, :, half] = placed
            q_recv[s, 0, half] = placed[0]

    def send_queries(s):
        def one(i, carry):
            dz, dx = offset(NW - i)
            o = dz * NX + dx
            pltpu.make_async_remote_copy(
                src_ref=q_send.at[s, o], dst_ref=q_recv.at[s, o], send_sem=qs.at[s],
                recv_sem=qr.at[s], device_id=ahead(dz, dx), device_id_type=MESH,
            ).start()
            return carry

        lax.fori_loop(1, NW, one, 0)

    def send_results(s, half=None):
        part = pl.ds(0, 2) if half is None else pl.ds(half, 1)

        def one(i, carry):
            dz, dx = offset(NW - i)
            o = dz * NX + dx
            pltpu.make_async_remote_copy(
                src_ref=r_send.at[s, o, part], dst_ref=r_recv.at[s, o, part],
                send_sem=rs.at[s + (half or 0)], recv_sem=rr.at[s + (half or 0)],
                device_id=behind(dz, dx), device_id_type=MESH,
            ).start()
            return carry

        lax.fori_loop(1, NW, one, 0)

    def send_early_logs():
        def one(i, carry):
            dz, dx = offset(NW - i)
            o = dz * NX + dx
            pltpu.make_async_remote_copy(
                src_ref=f_send.at[o], dst_ref=f_recv.at[o], send_sem=fs,
                recv_sem=fr, device_id=ahead(dz, dx), device_id_type=MESH,
            ).start()
            return carry

        lax.fori_loop(1, NW, one, 0)

    def send_projected(s):
        def one(i, carry):
            dz, dx = offset(NW - i)
            o = dz * NX + dx
            pltpu.make_async_remote_copy(
                src_ref=p_send.at[s, o], dst_ref=p_recv.at[s, o], send_sem=ps.at[s],
                recv_sem=pr.at[s], device_id=behind(dz, dx), device_id_type=MESH,
            ).start()
            return carry

        lax.fori_loop(1, NW, one, 0)

    def send_logs(s):
        def one(i, carry):
            dz, dx = offset(NW - i)
            o = dz * NX + dx
            pltpu.make_async_remote_copy(
                src_ref=l_send.at[s, o], dst_ref=l_recv.at[s, o], send_sem=ls.at[s],
                recv_sem=lr.at[s], device_id=behind(dz, dx), device_id_type=MESH,
            ).start()
            return carry

        lax.fori_loop(1, NW, one, 0)

    def await_all(ref, sem):
        pltpu.make_async_copy(ref, ref, sem).wait()

    dispatch(0)
    pl.semaphore_wait(barrier, NW - 1 + NY - 1 + 1)
    send_queries(0)
    for load in loads[STEPS:]:
        load.start()
    dispatch(1)
    send_queries(1)

    tables[1].wait()
    len_col[...] = jnp.broadcast_to(upright(len_ref[...]), (REQ, HD))
    for load in loads[6:10]:
        load.wait()
    loads[2].wait()
    loads[3].wait()
    qf[...] = q[...].astype(F32)
    nkf[...] = nk[...].astype(F32)
    nvf[...] = nv[...].astype(F32)
    kloc[LKEYS:] = jnp.zeros((HD, HD), BF16)
    vloc[LKEYS:, :HD] = jnp.zeros((HD, HD), BF16)
    vloc[:, HD:] = jnp.ones((LKEYS + HD, HD), BF16)
    own_i = lax.broadcasted_iota(I32, (BLOCK, LKEYS), 0)
    own_k = lax.broadcasted_iota(I32, (BLOCK, LKEYS), 1)
    own_hit = lax.shift_right_logical(own_k, 6) == own_i
    own_j = lax.bitwise_and(own_k, SUF - 1)
    new_s = lax.broadcasted_iota(I32, (STEPS, BLOCK, HD), 0)
    new_i = lax.broadcasted_iota(I32, (STEPS, BLOCK, HD), 1)
    new_k = lax.broadcasted_iota(I32, (STEPS, BLOCK, HD), 2)
    new_hit = (lax.bitwise_and(new_k, BLOCK - 1) == new_i) & (
        lax.shift_right_logical(new_k, 3) <= new_s
    )

    def local_block(b, carry):
        rows = pl.ds(pl.multiple_of(b * BLOCK, BLOCK), BLOCK)
        query = jnp.concatenate(
            [qf[s, rows, h * HD:(h + 1) * HD] for s in range(STEPS) for h in range(HL)], axis=0
        ).astype(BF16)
        kloc[:LKEYS] = sk[rows].reshape(LKEYS, HD)
        vloc[:LKEYS, :HD] = sv[rows].reshape(LKEYS, HD)
        kloc[LKEYS:LKEYS + STEPS * BLOCK] = nkf[:, rows, :].reshape(STEPS * BLOCK, HD).astype(BF16)
        vloc[LKEYS:LKEYS + STEPS * BLOCK, :HD] = (
            nvf[:, rows, :].reshape(STEPS * BLOCK, HD).astype(BF16)
        )
        length = len_col[rows, :1]
        past = dot_t(query, kloc[:LKEYS]).reshape(STEPS * HL, BLOCK, LKEYS)
        past = jnp.where((own_hit & (own_j < length))[None], past, -jnp.inf)
        fresh = dot_t(query, kloc[LKEYS:]).reshape(STEPS, HL, BLOCK, HD)
        fresh = jnp.where(new_hit[:, None], fresh, -jnp.inf)
        past = past.reshape(STEPS * HL * BLOCK, LKEYS)
        fresh = fresh.reshape(STEPS * HL * BLOCK, HD)
        top = jnp.maximum(
            jnp.max(past, axis=-1, keepdims=True), jnp.max(fresh, axis=-1, keepdims=True)
        )
        past = jnp.exp2((past - top) * (SCALE * LOG2E)).astype(BF16)
        fresh = jnp.exp2((fresh - top) * (SCALE * LOG2E)).astype(BF16)
        both = dot(past, vloc[:LKEYS]) + dot(fresh, vloc[LKEYS:])
        total = both[:, HD:]
        shape = (STEPS, HL, BLOCK, HD)
        loc_out[:, :, rows, :] = (both[:, :HD] / total).reshape(shape)
        loc_log[:, :, rows, :] = (top * SCALE + jnp.log(total)).reshape(shape)
        return carry

    lax.fori_loop(0, REQ // BLOCK, local_block, 0)

    own = jnp.broadcast_to(lax.shift_right_logical(slot_col, 4), (REQ, HD))
    pick = lax.bitwise_and(slot_col, 8) * 2 + lax.bitwise_and(slot_col, 1)
    lanes = lax.broadcasted_iota(I32, (REQ, HD), 1)

    logs_out = jnp.zeros((REQ, HD), F32)
    for e in range(EARLY):
        for h in range(HL):
            logs_out = jnp.where(lanes == pick + (e * 32 + 2 * h), loc_log[FIRST + e, h], logs_out)
    for o in range(NW):
        row = jnp.sum(jnp.where(own == o, logs_out, 0.0), axis=0, keepdims=True)
        f_send[o] = row
        if o == 0:
            f_recv[o] = row
    send_early_logs()
    dispatch(2)
    send_queries(2)
    dispatch(3)
    send_queries(3)

    tall_sub = lax.broadcasted_iota(I32, (HALF, REQ), 0)
    tall_lane = lax.broadcasted_iota(I32, (HALF, REQ), 1)
    key_col = jnp.sum(
        jnp.where(lax.bitwise_and(tall_sub, REQ - 1) == tall_lane, slot, 0),
        axis=1, keepdims=True,
    ) + 2 * lax.shift_right_logical(lax.broadcasted_iota(I32, (HALF, 1), 0), 6)
    hit = lax.broadcasted_iota(I32, (HALF, ROWS), 1) == key_col
    gather[...] = jnp.where(hit, 1.0, 0.0).astype(BF16)
    slot_out = (
        lax.shift_left(lax.shift_right_logical(slot, 4), 4)
        + lax.shift_right_logical(lax.bitwise_and(slot, 8), 2) + lax.bitwise_and(slot, 1)
    )
    key_out = jnp.sum(
        jnp.where(lax.bitwise_and(tall_sub, REQ - 1) == tall_lane, slot_out, 0),
        axis=1, keepdims=True,
    ) + 4 * lax.shift_right_logical(lax.broadcasted_iota(I32, (HALF, 1), 0), 6)
    hit = lax.broadcasted_iota(I32, (HALF, ROWS), 1) == key_out
    pick_out[...] = jnp.where(hit, 1.0, 0.0).astype(BF16)
    at = lax.broadcasted_iota(I32, (ROWS, 1), 0)
    column = lax.broadcasted_iota(I32, (ROWS, ROWS), 1)
    turn = lax.bitwise_and(at, 1)
    target = (
        lax.bitwise_and(lax.shift_right_logical(at, 1), NW - 1) * 16
        + lax.shift_right_logical(at, 6) * 2 + turn
    )
    order_in[...] = jnp.where(column == target, 1.0, 0.0).astype(BF16)
    target = (
        lax.bitwise_and(lax.shift_right_logical(at, 2), 3) * 128
        + lax.bitwise_and(lax.shift_right_logical(at, 1), 1) * 64
        + lax.shift_right_logical(at, 4) * 2 + turn
    )
    order_out[...] = jnp.where(column == target, 1.0, 0.0).astype(BF16)
    loads[4].wait()
    loads[5].wait()
    vones[:, :, :HD] = pv[...]
    vones[:, :, HD:] = jnp.ones((2, PRE, HD), BF16)


    log_lane = lax.broadcasted_iota(I32, (1, 2 * HL, HD), 2)
    place = lax.broadcasted_iota(I32, (1, 2 * HL, HD), 1)
    PART = 16

    def attend(s):
        await_all(q_recv.at[s, pl.ds(1, NW - 1)], qr.at[s])

        def part(i, carry):
            some = pl.ds(i * PART, PART)
            logs = jnp.zeros((PART, 2 * HL, HD), F32)
            arrived = q_recv[s, some].astype(F32)
            results = []
            for p in range(2):
                rows = slice(p * 8, p * 8 + 8)
                query = jnp.concatenate([arrived[:, 0, rows], arrived[:, 1, rows]], axis=1)
                scores = dot_t(query.astype(BF16).reshape(PART * 2 * HL, HD), pk[p])
                top = jnp.max(scores, axis=-1, keepdims=True)
                weights = jnp.exp2((scores - top) * (SCALE * LOG2E)).astype(BF16)
                both = dot(weights, vones[p])
                total = both[:, HD:]
                result = (both[:, :HD] / total).reshape(PART, 2 * HL, HD)
                log = (top * SCALE + jnp.log(total)).reshape(PART, 2 * HL, HD)
                if is_early(s):
                    there = jnp.where(
                        log_lane == place + ((s - FIRST) * 32 + p * 2 * HL), f_recv[some], 0.0
                    )
                    there = jnp.sum(there, axis=-1, keepdims=True)
                    high = jnp.maximum(log, there)
                    a, b = jnp.exp(log - high), jnp.exp(there - high)
                    raw[p, some] = (result * (a / (a + b))).astype(BF16)
                results.append(result)
                logs = jnp.where(log_lane == place + p * 2 * HL, log, logs)
            for half in range(0 if is_early(s) else 2):
                rows = slice(half * 8, half * 8 + 8)
                r_send[s, some, half] = jnp.concatenate(
                    [results[0][:, rows], results[1][:, rows]], axis=1
                ).astype(BF16)
            l_send[s, some] = jnp.sum(logs, axis=1, keepdims=True)
            return carry

        lax.fori_loop(0, NW // PART, part, 0)
        l_recv[s, 0] = l_send[s, 0]
        send_logs(s)
        if is_early(s):
            for p in range(2):
                moved = dot(order_in[...], raw[p].reshape(ROWS, HD)).astype(BF16)
                for h in range(HL):
                    slot_attn[p, :, h * HD:(h + 1) * HD] = moved[h * REQ:(h + 1) * REQ]
            return
        r_recv[s, 0] = r_send[s, 0]
        if s == LAST:
            send_results(s, 0)
            send_results(s, 1)
        else:
            send_results(s)

    def merge(s):
        await_all(l_recv.at[s, pl.ds(1, NW - 1)], lr.at[s])
        logs = jnp.zeros((REQ, HD), F32)
        for o in range(NW):
            logs = jnp.where(own == o, l_recv[s, o], logs)
        for h in range(HL):
            pre = jnp.sum(jnp.where(lanes == pick + 2 * h, logs, 0.0), axis=1, keepdims=True)
            loc = loc_log[s, h]
            high = jnp.maximum(pre, loc)
            a, b = jnp.exp(pre - high), jnp.exp(loc - high)
            mine = loc_out[s, h] * (b / (a + b))
            if is_early(s):
                attn[s, :, h * HD:(h + 1) * HD] = mine.astype(BF16)
            else:
                pre_part[h] = a / (a + b)
                loc_out[s, h] = mine

    def take(s, half):
        back = dot(gather[...], r_recv[s, :, half].reshape(ROWS, HD))
        for n in range(4):
            h = half * 4 + n
            joint = pre_part[h] * back[n * REQ:(n + 1) * REQ] + loc_out[s, h]
            attn[s, :, h * HD:(h + 1) * HD] = joint.astype(BF16)

    def block(dy, core):
        return lax.rem(y + dy, NY) * 2 + core

    WIDE = HL * HD // 2

    def term(s, dy, side):
        n = block(dy, 1 - c if side else c)
        if s == LAST:
            return early[dy, side] + dot(attn[s, :, WIDE:], w[n, WIDE:])
        return dot(attn[s], w[n])

    def begin(s):
        for side in (1, 0):
            for dy in (2, 1, 3, 0):
                n = block(dy, 1 - c if side else c)
                early[dy, side] = dot(attn[s, :, :WIDE], w[n, :WIDE])

    def give(s, dy):
        given[s, dy] = term(s, dy, 1).astype(BF16)
        pltpu.make_async_remote_copy(
            src_ref=given.at[s, dy], dst_ref=c_recv.at[s, dy], send_sem=cs.at[s, dy],
            recv_sem=cr.at[s, dy], device_id=other, device_id_type=MESH,
        ).start()

    def keep(s, dy):
        kept[s, dy] = term(s, dy, 0)

    def pair(s, dy):
        await_all(c_recv.at[s, dy], cr.at[s, dy])
        both = kept[s, dy] + c_recv[s, dy].astype(F32)
        if dy == 0:
            kept[s, dy] = both
            pltpu.make_async_copy(kept.at[s, dy], own_hbm.at[s], out_sems.at[s]).start()
            return
        y_send[s, dy - 1] = both.astype(BF16)
        pltpu.make_async_remote_copy(
            src_ref=y_send.at[s, dy - 1], dst_ref=y_recv.at[dy - 1, s],
            send_sem=ys.at[s], recv_sem=yr.at[s], device_id=across(dy), device_id_type=MESH,
        ).start()

    def project(s):
        give(s, 2)
        give(s, 1)
        give(s, 3)
        keep(s, 2)
        keep(s, 1)
        pair(s, 2)
        keep(s, 3)
        pair(s, 1)
        give(s, 0)
        pair(s, 3)
        keep(s, 0)
        pair(s, 0)

    def rows_of(u):
        if u < EARLY:
            return slot_attn[...].reshape(2 * REQ, HL * HD)
        return attn[FIRST:FIRST + EARLY].reshape(2 * REQ, HL * HD)

    def give_early(u, dy):
        term = dot(rows_of(u), w[block(dy, 1 - c)]).astype(BF16)
        given_e[u, dy] = term.reshape(2, REQ, SHARE)
        pltpu.make_async_remote_copy(
            src_ref=given_e.at[u, dy], dst_ref=c_recv_e.at[u, dy], send_sem=cse.at[u, dy],
            recv_sem=cre.at[u, dy], device_id=other, device_id_type=MESH,
        ).start()

    def keep_early(u, dy):
        kept_e[u, dy] = dot(rows_of(u), w[block(dy, c)]).reshape(2, REQ, SHARE)

    def pair_early(u, dy):
        await_all(c_recv_e.at[u, dy], cre.at[u, dy])
        both = kept_e[u, dy] + c_recv_e[u, dy].astype(F32)
        if dy == 0:
            kept_e[u, dy] = both
            return
        y_send_e[u, dy - 1] = both.astype(BF16)
        target = y_recv_e.at[u, dy - 1] if u < EARLY else y_recv.at[dy - 1, pl.ds(FIRST, EARLY)]
        pltpu.make_async_remote_copy(
            src_ref=y_send_e.at[u, dy - 1], dst_ref=target, send_sem=yse.at[u],
            recv_sem=yre.at[u], device_id=across(dy), device_id_type=MESH,
        ).start()

    def project_early(u):
        give_early(u, 2)
        give_early(u, 1)
        give_early(u, 3)
        keep_early(u, 2)
        keep_early(u, 1)
        pair_early(u, 2)
        keep_early(u, 3)
        pair_early(u, 1)
        give_early(u, 0)
        pair_early(u, 3)
        keep_early(u, 0)
        pair_early(u, 0)

    def return_early(s):
        await_all(y_recv_e.at[s], yre.at[s])
        total = kept_e[s, 0]
        for dy in range(NY - 1):
            total = total + y_recv_e[s, dy].astype(F32)
        total = total.astype(BF16).reshape(2 * REQ, SHARE)
        stacked = jnp.concatenate([total[:, j * HD:(j + 1) * HD] for j in range(4)], axis=0)
        placed = dot(order_out[...], stacked).astype(BF16).reshape(NW, 16, HD)
        p_send[s] = placed
        p_recv[s, 0] = placed[0]
        send_projected(s)

    def combine_early(s):
        await_all(p_recv.at[s, pl.ds(1, NW - 1)], pr.at[s])
        back = dot(pick_out[...], p_recv[s].reshape(ROWS, HD))
        for j in range(4):
            cols = slice(j * HD, (j + 1) * HD)
            own_v[s, :, cols] = kept_e[EARLY, 0, s, :, cols] + back[j * REQ:(j + 1) * REQ]
        pltpu.make_async_copy(own_v.at[s], own_hbm.at[FIRST + s], out_sems.at[FIRST + s]).start()

    def step(s):
        merge(s)
        if s == LAST:
            for half in range(2):
                await_all(r_recv.at[s, pl.ds(1, NW - 1), half], rr.at[s + half])
                take(s, half)
                if half == 0:
                    begin(s)
        else:
            await_all(r_recv.at[s, pl.ds(1, NW - 1)], rr.at[s])
            take(s, 0)
            take(s, 1)
        project(s)

    attend(0)
    await_all(f_recv.at[pl.ds(1, NW - 1)], fr)
    attend(1)
    for load in loads[10:]:
        load.wait()
    project_early(0)
    attend(2)
    project_early(1)
    return_early(0)
    attend(3)
    merge(1)
    merge(2)
    project_early(2)
    step(0)
    return_early(1)
    combine_early(0)
    step(3)
    combine_early(1)

    await_all(f_send.at[pl.ds(1, NW - 1)], fs)
    for u in range(EARLY + 1):
        for dy in range(NY):
            await_all(given_e.at[u, dy], cse.at[u, dy])
        await_all(y_send_e.at[u], yse.at[u])
    await_all(y_recv.at[:, pl.ds(FIRST, EARLY)], yre.at[EARLY])
    for s in range(EARLY):
        await_all(p_send.at[s, pl.ds(1, NW - 1)], ps.at[s])
        pltpu.make_async_copy(own_v.at[s], own_hbm.at[FIRST + s], out_sems.at[FIRST + s]).wait()
    for s in range(STEPS):
        await_all(q_send.at[s, pl.ds(1, NW - 1)], qs.at[s])
        await_all(l_send.at[s, pl.ds(1, NW - 1)], ls.at[s])
        if is_early(s):
            continue
        if s == LAST:
            for half in range(2):
                await_all(r_send.at[s, pl.ds(1, NW - 1), half], rs.at[s + half])
        else:
            await_all(r_send.at[s, pl.ds(1, NW - 1)], rs.at[s])
        for dy in range(NY):
            await_all(given.at[s, dy], cs.at[s, dy])
        await_all(y_send.at[s], ys.at[s])
        pltpu.make_async_copy(kept.at[s, 0], own_hbm.at[s], out_sems.at[s]).wait()
    for s in range(STEPS):
        if not is_early(s):
            await_all(y_recv.at[:, s], yr.at[s])


def body(
    queries, new_keys, new_values, suffix_keys, suffix_values, suffix_len,
    prefix_keys, prefix_values, prefix_of, out_weight,
):
    anywhere = pl.BlockSpec(memory_space=pl.ANY)
    fixed = functools.partial(pltpu.with_memory_space_constraint, memory_space=pltpu.HBM)
    dma = pltpu.SemaphoreType.DMA
    slots = (STEPS, NW, 2, 16, HD)
    logs = (STEPS, NW, 1, HD)
    own, parts = pl.pallas_call(
        kernel,
        out_shape=(
            jax.ShapeDtypeStruct((STEPS, REQ, SHARE), F32),
            jax.ShapeDtypeStruct((NY - 1, STEPS, REQ, SHARE), BF16),
        ),
        in_specs=[anywhere] * 10,
        out_specs=(anywhere, anywhere),
        scratch_shapes=[
            pltpu.VMEM(queries.shape, BF16),
            pltpu.VMEM(new_keys.shape, BF16),
            pltpu.VMEM(new_values.shape, BF16),
            pltpu.VMEM(suffix_keys.shape, BF16),
            pltpu.VMEM(suffix_values.shape, BF16),
            pltpu.VMEM(prefix_keys.shape, BF16),
            pltpu.VMEM(prefix_values.shape, BF16),
            pltpu.VMEM((2 * NY, out_weight.shape[0], SHARE), BF16),
            pltpu.VMEM((2, PRE, 2 * HD), BF16),
            pltpu.VMEM(queries.shape, F32),
            pltpu.VMEM(new_keys.shape, F32),
            pltpu.VMEM(new_values.shape, F32),
            pltpu.VMEM((LKEYS + HD, HD), BF16),
            pltpu.VMEM((LKEYS + HD, 2 * HD), BF16),
            pltpu.VMEM((1, REQ), I32),
            pltpu.VMEM((1, REQ), I32),
            pltpu.VMEM((REQ, HD), I32),
            pltpu.VMEM((ROWS, HALF), BF16),
            pltpu.VMEM((HALF, ROWS), BF16),
            pltpu.VMEM(slots, BF16),
            pltpu.VMEM(slots, BF16),
            pltpu.VMEM(slots, BF16),
            pltpu.VMEM(slots, BF16),
            pltpu.VMEM(logs, F32),
            pltpu.VMEM(logs, F32),
            pltpu.VMEM((STEPS, HL, REQ, HD), F32),
            pltpu.VMEM((STEPS, HL, REQ, HD), F32),
            pltpu.VMEM((HL, REQ, HD), F32),
            pltpu.VMEM((STEPS, REQ, HL * HD), BF16),
            pltpu.VMEM((NY, 2, REQ, SHARE), F32),
            pltpu.VMEM((STEPS, NY, REQ, SHARE), F32),
            pltpu.VMEM((STEPS, NY, REQ, SHARE), BF16),
            pltpu.VMEM((STEPS, NY, REQ, SHARE), BF16),
            pltpu.VMEM((STEPS, NY - 1, REQ, SHARE), BF16),
            pltpu.VMEM((ROWS, ROWS), BF16),
            pltpu.VMEM((ROWS, ROWS), BF16),
            pltpu.VMEM((HALF, ROWS), BF16),
            pltpu.VMEM((NW, 1, HD), F32),
            pltpu.VMEM((NW, 1, HD), F32),
            pltpu.VMEM((2, NW, 16, HD), BF16),
            pltpu.VMEM((2, REQ, HL * HD), BF16),
            pltpu.VMEM((EARLY + 1, NY, 2, REQ, SHARE), F32),
            pltpu.VMEM((EARLY + 1, NY, 2, REQ, SHARE), BF16),
            pltpu.VMEM((EARLY + 1, NY, 2, REQ, SHARE), BF16),
            pltpu.VMEM((EARLY + 1, NY - 1, 2, REQ, SHARE), BF16),
            pltpu.VMEM((EARLY, NY - 1, 2, REQ, SHARE), BF16),
            pltpu.VMEM((EARLY, NW, 16, HD), BF16),
            pltpu.VMEM((EARLY, NW, 16, HD), BF16),
            pltpu.VMEM((EARLY, REQ, SHARE), F32),
            dma((STEPS + 8 + 2 * NY,)),
            dma((STEPS,)),
        ] + [dma((STEPS,))] * 2 + [dma((STEPS + 1,))] * 2 + [dma((STEPS,))] * 2 + [dma((STEPS, NY))] * 2 + [dma((STEPS,))] * 2
        + [dma, dma] + [dma((EARLY + 1, NY))] * 2 + [dma((EARLY + 1,))] * 2 + [dma((EARLY,))] * 2,
        compiler_params=pltpu.CompilerParams(
            collective_id=0, has_side_effects=True, vmem_limit_bytes=48 * 2**20
        ),
        name="attention",
    )(
        fixed(queries), fixed(prefix_of.reshape(1, REQ)), fixed(suffix_len.reshape(1, REQ)),
        *(
            fixed(a)
            for a in (new_keys, new_values, suffix_keys, suffix_values,
                      prefix_keys, prefix_values, out_weight)
        ),
    )
    for dy in range(NY - 1):
        own = own + parts[dy].astype(F32)
    return own.astype(BF16)


def solution(mesh):
    return jax.shard_map(
        body,
        mesh=mesh,
        in_specs=(
            P(None, "wide", "tensor"),
            P(None, "wide", "tensor"),
            P(None, "wide", "tensor"),
            P("wide", None, "tensor"),
            P("wide", None, "tensor"),
            P("wide"),
            P("wide", None, "tensor"),
            P("wide", None, "tensor"),
            P("wide", None),
            P("tensor", None),
        ),
        out_specs=P(None, "wide", "tensor"),
        check_vma=False,
    )
```

```python
import functools

import jax
import jax.numpy as jnp
from jax import lax
from jax.experimental import pallas as pl
from jax.experimental.pallas import tpu as pltpu
from jax.sharding import PartitionSpec as P

MESH = pl.DeviceIdType.MESH
HD = 128
NZ, NX, NY = 8, 4, 4
NW = NZ * NX
STEPS, REQ, HL = 4, 64, 8
PRE, SUF = 768, 64
ROWS = HL * REQ
HALF = ROWS // 2
LAST = STEPS - 1
EARLY = 2
FIRST = 1
SCALE = HD ** (-0.5)
LOG2E = 1.4426950408889634
BLOCK = 8
LKEYS = BLOCK * SUF
DOUT = 4096
SHARE = 512
F32, BF16, I32 = jnp.float32, jnp.bfloat16, jnp.int32


def is_early(s):
    return FIRST <= s < FIRST + EARLY


def dot(a, b):
    return lax.dot_general(a, b, (((1,), (0,)), ((), ())), preferred_element_type=F32)


def dot_t(a, b):
    return lax.dot_general(a, b, (((1,), (1,)), ((), ())), preferred_element_type=F32)


def kernel(
    q_hbm, pof_hbm, len_hbm, nk_hbm, nv_hbm, sk_hbm, sv_hbm, pk_hbm, pv_hbm, w_hbm,
    own_hbm, y_recv,
    q, nk, nv, sk, sv, pk, pv, w, vones, qf, nkf, nvf, kloc, vloc,
    pof_ref, len_ref, len_col,
    spread, gather, q_send, q_recv, r_send, r_recv, l_send, l_recv,
    loc_out, loc_log, pre_part, attn, kept, given, c_recv, y_send,
    order_in, order_out, pick_out, f_send, f_recv, raw, slot_attn, kept_e, given_e, c_recv_e,
    y_send_e, y_recv_e, p_send, p_recv, own_v,
    in_sems, out_sems, qs, qr, rs, rr, ls, lr, cs, cr, ys, yr, fs, fr, cse, cre, yse, yre, ps, pr,
):
    me_w, me_t = lax.axis_index("wide"), lax.axis_index("tensor")
    z, x = me_w // NX, me_w % NX
    y, c = me_t // 2, me_t % 2

    def offset(i):
        zi = i // NX
        half = (zi + 1) // 2
        dz = lax.rem(jnp.where(lax.rem(zi, 2) == 1, half, NZ - half), NZ)
        return dz, lax.rem(i, NX)

    def ahead(dz, dx):
        return (lax.rem(z + dz, NZ) * NX + lax.rem(x + dx, NX), me_t)

    def behind(dz, dx):
        return (lax.rem(z + NZ - dz, NZ) * NX + lax.rem(x + NX - dx, NX), me_t)

    def across(dy):
        return (me_w, lax.rem(y + dy, NY) * 2 + c)

    other = (me_w, y * 2 + 1 - c)

    loads = [
        pltpu.make_async_copy(src, dst, in_sems.at[n])
        for n, (src, dst) in enumerate(
            [(q_hbm.at[s], q.at[s]) for s in range(STEPS)]
            + [(pk_hbm, pk), (pv_hbm, pv), (nk_hbm, nk), (nv_hbm, nv), (sk_hbm, sk), (sv_hbm, sv)]
            + [(w_hbm.at[:, pl.ds(n * SHARE, SHARE)], w.at[n]) for n in range(2 * NY)]
        )
    ]
    tables = [
        pltpu.make_async_copy(src, dst, in_sems.at[len(loads) + n])
        for n, (src, dst) in enumerate([(pof_hbm, pof_ref), (len_hbm, len_ref)])
    ]
    for load in tables + loads[:STEPS]:
        load.start()

    barrier = pltpu.get_barrier_semaphore()

    def greet(i, carry):
        pl.semaphore_signal(barrier, inc=1, device_id=ahead(*offset(i)), device_id_type=MESH)
        return carry

    lax.fori_loop(1, NW, greet, 0)
    for dy in range(1, NY):
        pl.semaphore_signal(barrier, inc=1, device_id=across(dy), device_id_type=MESH)
    pl.semaphore_signal(barrier, inc=1, device_id=other, device_id_type=MESH)

    tables[0].wait()
    pof = pof_ref[...]
    sub = lax.broadcasted_iota(I32, (REQ, REQ), 0)
    lane = lax.broadcasted_iota(I32, (REQ, REQ), 1)

    def upright(row):
        return jnp.sum(jnp.where(sub == lane, row, 0), axis=1, keepdims=True)

    rank = jnp.sum(
        jnp.where((upright(pof) == pof) & (sub < lane), 1, 0), axis=0, keepdims=True
    )
    owner = lax.shift_right_logical(pof, 1)
    dz = lax.bitwise_and(lax.shift_right_logical(owner, 2) - z + NZ, NZ - 1)
    dx = lax.bitwise_and(lax.bitwise_and(owner, NX - 1) - x + NX, NX - 1)
    slot = (dz * NX + dx) * 16 + lax.bitwise_and(pof, 1) * 8 + rank
    slot_col = upright(slot)
    wide_sub = lax.broadcasted_iota(I32, (REQ, HALF), 0)
    wide_lane = lax.broadcasted_iota(I32, (REQ, HALF), 1)
    key_row = jnp.sum(
        jnp.where(wide_sub == lax.bitwise_and(wide_lane, REQ - 1), slot_col, 0),
        axis=0, keepdims=True,
    ) + 2 * lax.shift_right_logical(lax.broadcasted_iota(I32, (1, HALF), 1), 6)
    hit = lax.broadcasted_iota(I32, (ROWS, HALF), 0) == key_row
    spread[...] = jnp.where(hit, 1.0, 0.0).astype(BF16)

    def dispatch(s):
        if s < 2:
            loads[s].wait()
        for half in range(2):
            stacked = jnp.concatenate(
                [q[s, :, h * HD:(h + 1) * HD] for h in range(half * 4, half * 4 + 4)], axis=0
            )
            placed = dot(spread[...], stacked).astype(BF16).reshape(NW, 16, HD)
            q_send[s, :, half] = placed
            q_recv[s, 0, half] = placed[0]

    def send_queries(s):
        def one(i, carry):
            dz, dx = offset(NW - i)
            o = dz * NX + dx
            pltpu.make_async_remote_copy(
                src_ref=q_send.at[s, o], dst_ref=q_recv.at[s, o], send_sem=qs.at[s],
                recv_sem=qr.at[s], device_id=ahead(dz, dx), device_id_type=MESH,
            ).start()
            return carry

        lax.fori_loop(1, NW, one, 0)

    def send_results(s):
        def one(i, carry):
            dz, dx = offset(NW - i)
            o = dz * NX + dx
            pltpu.make_async_remote_copy(
                src_ref=r_send.at[s, o], dst_ref=r_recv.at[s, o], send_sem=rs.at[s],
                recv_sem=rr.at[s], device_id=behind(dz, dx), device_id_type=MESH,
            ).start()
            return carry

        lax.fori_loop(1, NW, one, 0)

    def send_early_logs():
        def one(i, carry):
            dz, dx = offset(NW - i)
            o = dz * NX + dx
            pltpu.make_async_remote_copy(
                src_ref=f_send.at[o], dst_ref=f_recv.at[o], send_sem=fs,
                recv_sem=fr, device_id=ahead(dz, dx), device_id_type=MESH,
            ).start()
            return carry

        lax.fori_loop(1, NW, one, 0)

    def send_projected(s):
        def one(i, carry):
            dz, dx = offset(NW - i)
            o = dz * NX + dx
            pltpu.make_async_remote_copy(
                src_ref=p_send.at[s, o], dst_ref=p_recv.at[s, o], send_sem=ps.at[s],
                recv_sem=pr.at[s], device_id=behind(dz, dx), device_id_type=MESH,
            ).start()
            return carry

        lax.fori_loop(1, NW, one, 0)

    def send_logs(s):
        def one(i, carry):
            dz, dx = offset(NW - i)
            o = dz * NX + dx
            pltpu.make_async_remote_copy(
                src_ref=l_send.at[s, o], dst_ref=l_recv.at[s, o], send_sem=ls.at[s],
                recv_sem=lr.at[s], device_id=behind(dz, dx), device_id_type=MESH,
            ).start()
            return carry

        lax.fori_loop(1, NW, one, 0)

    def await_all(ref, sem):
        pltpu.make_async_copy(ref, ref, sem).wait()

    dispatch(0)
    pl.semaphore_wait(barrier, NW - 1 + NY - 1 + 1)
    send_queries(0)
    for load in loads[STEPS:]:
        load.start()
    dispatch(1)
    send_queries(1)

    tables[1].wait()
    len_col[...] = jnp.broadcast_to(upright(len_ref[...]), (REQ, HD))
    for load in loads[6:10]:
        load.wait()
    loads[2].wait()
    loads[3].wait()
    qf[...] = q[...].astype(F32)
    nkf[...] = nk[...].astype(F32)
    nvf[...] = nv[...].astype(F32)
    kloc[LKEYS:] = jnp.zeros((HD, HD), BF16)
    vloc[LKEYS:, :HD] = jnp.zeros((HD, HD), BF16)
    vloc[:, HD:] = jnp.ones((LKEYS + HD, HD), BF16)
    own_i = lax.broadcasted_iota(I32, (BLOCK, LKEYS), 0)
    own_k = lax.broadcasted_iota(I32, (BLOCK, LKEYS), 1)
    own_hit = lax.shift_right_logical(own_k, 6) == own_i
    own_j = lax.bitwise_and(own_k, SUF - 1)
    new_s = lax.broadcasted_iota(I32, (STEPS, BLOCK, HD), 0)
    new_i = lax.broadcasted_iota(I32, (STEPS, BLOCK, HD), 1)
    new_k = lax.broadcasted_iota(I32, (STEPS, BLOCK, HD), 2)
    new_hit = (lax.bitwise_and(new_k, BLOCK - 1) == new_i) & (
        lax.shift_right_logical(new_k, 3) <= new_s
    )

    def local_block(b, carry):
        rows = pl.ds(pl.multiple_of(b * BLOCK, BLOCK), BLOCK)
        query = jnp.concatenate(
            [qf[s, rows, h * HD:(h + 1) * HD] for s in range(STEPS) for h in range(HL)], axis=0
        ).astype(BF16)
        kloc[:LKEYS] = sk[rows].reshape(LKEYS, HD)
        vloc[:LKEYS, :HD] = sv[rows].reshape(LKEYS, HD)
        kloc[LKEYS:LKEYS + STEPS * BLOCK] = nkf[:, rows, :].reshape(STEPS * BLOCK, HD).astype(BF16)
        vloc[LKEYS:LKEYS + STEPS * BLOCK, :HD] = (
            nvf[:, rows, :].reshape(STEPS * BLOCK, HD).astype(BF16)
        )
        length = len_col[rows, :1]
        past = dot_t(query, kloc[:LKEYS]).reshape(STEPS * HL, BLOCK, LKEYS)
        past = jnp.where((own_hit & (own_j < length))[None], past, -jnp.inf)
        fresh = dot_t(query, kloc[LKEYS:]).reshape(STEPS, HL, BLOCK, HD)
        fresh = jnp.where(new_hit[:, None], fresh, -jnp.inf)
        past = past.reshape(STEPS * HL * BLOCK, LKEYS)
        fresh = fresh.reshape(STEPS * HL * BLOCK, HD)
        top = jnp.maximum(
            jnp.max(past, axis=-1, keepdims=True), jnp.max(fresh, axis=-1, keepdims=True)
        )
        past = jnp.exp2((past - top) * (SCALE * LOG2E)).astype(BF16)
        fresh = jnp.exp2((fresh - top) * (SCALE * LOG2E)).astype(BF16)
        both = dot(past, vloc[:LKEYS]) + dot(fresh, vloc[LKEYS:])
        total = both[:, HD:]
        shape = (STEPS, HL, BLOCK, HD)
        loc_out[:, :, rows, :] = (both[:, :HD] / total).reshape(shape)
        loc_log[:, :, rows, :] = (top * SCALE + jnp.log(total)).reshape(shape)
        return carry

    lax.fori_loop(0, REQ // BLOCK, local_block, 0)

    own = jnp.broadcast_to(lax.shift_right_logical(slot_col, 4), (REQ, HD))
    pick = lax.bitwise_and(slot_col, 8) * 2 + lax.bitwise_and(slot_col, 1)
    lanes = lax.broadcasted_iota(I32, (REQ, HD), 1)

    logs_out = jnp.zeros((REQ, HD), F32)
    for e in range(EARLY):
        for h in range(HL):
            logs_out = jnp.where(lanes == pick + (e * 32 + 2 * h), loc_log[FIRST + e, h], logs_out)
    for o in range(NW):
        row = jnp.sum(jnp.where(own == o, logs_out, 0.0), axis=0, keepdims=True)
        f_send[o] = row
        if o == 0:
            f_recv[o] = row
    send_early_logs()
    dispatch(2)
    send_queries(2)
    dispatch(3)
    send_queries(3)

    tall_sub = lax.broadcasted_iota(I32, (HALF, REQ), 0)
    tall_lane = lax.broadcasted_iota(I32, (HALF, REQ), 1)
    key_col = jnp.sum(
        jnp.where(lax.bitwise_and(tall_sub, REQ - 1) == tall_lane, slot, 0),
        axis=1, keepdims=True,
    ) + 2 * lax.shift_right_logical(lax.broadcasted_iota(I32, (HALF, 1), 0), 6)
    hit = lax.broadcasted_iota(I32, (HALF, ROWS), 1) == key_col
    gather[...] = jnp.where(hit, 1.0, 0.0).astype(BF16)
    slot_out = (
        lax.shift_left(lax.shift_right_logical(slot, 4), 4)
        + lax.shift_right_logical(lax.bitwise_and(slot, 8), 2) + lax.bitwise_and(slot, 1)
    )
    key_out = jnp.sum(
        jnp.where(lax.bitwise_and(tall_sub, REQ - 1) == tall_lane, slot_out, 0),
        axis=1, keepdims=True,
    ) + 4 * lax.shift_right_logical(lax.broadcasted_iota(I32, (HALF, 1), 0), 6)
    hit = lax.broadcasted_iota(I32, (HALF, ROWS), 1) == key_out
    pick_out[...] = jnp.where(hit, 1.0, 0.0).astype(BF16)
    at = lax.broadcasted_iota(I32, (ROWS, 1), 0)
    column = lax.broadcasted_iota(I32, (ROWS, ROWS), 1)
    turn = lax.bitwise_and(at, 1)
    target = (
        lax.bitwise_and(lax.shift_right_logical(at, 1), NW - 1) * 16
        + lax.shift_right_logical(at, 6) * 2 + turn
    )
    order_in[...] = jnp.where(column == target, 1.0, 0.0).astype(BF16)
    target = (
        lax.bitwise_and(lax.shift_right_logical(at, 2), 3) * 128
        + lax.bitwise_and(lax.shift_right_logical(at, 1), 1) * 64
        + lax.shift_right_logical(at, 4) * 2 + turn
    )
    order_out[...] = jnp.where(column == target, 1.0, 0.0).astype(BF16)
    loads[4].wait()
    loads[5].wait()
    vones[:, :, :HD] = pv[...]
    vones[:, :, HD:] = jnp.ones((2, PRE, HD), BF16)


    log_lane = lax.broadcasted_iota(I32, (1, 2 * HL, HD), 2)
    place = lax.broadcasted_iota(I32, (1, 2 * HL, HD), 1)
    PART = 16

    def attend(s):
        await_all(q_recv.at[s, pl.ds(1, NW - 1)], qr.at[s])

        def part(i, carry):
            some = pl.ds(i * PART, PART)
            logs = jnp.zeros((PART, 2 * HL, HD), F32)
            arrived = q_recv[s, some].astype(F32)
            results = []
            for p in range(2):
                rows = slice(p * 8, p * 8 + 8)
                query = jnp.concatenate([arrived[:, 0, rows], arrived[:, 1, rows]], axis=1)
                scores = dot_t(query.astype(BF16).reshape(PART * 2 * HL, HD), pk[p])
                top = jnp.max(scores, axis=-1, keepdims=True)
                weights = jnp.exp2((scores - top) * (SCALE * LOG2E)).astype(BF16)
                both = dot(weights, vones[p])
                total = both[:, HD:]
                result = (both[:, :HD] / total).reshape(PART, 2 * HL, HD)
                log = (top * SCALE + jnp.log(total)).reshape(PART, 2 * HL, HD)
                if is_early(s):
                    there = jnp.where(
                        log_lane == place + ((s - FIRST) * 32 + p * 2 * HL), f_recv[some], 0.0
                    )
                    there = jnp.sum(there, axis=-1, keepdims=True)
                    high = jnp.maximum(log, there)
                    a, b = jnp.exp(log - high), jnp.exp(there - high)
                    raw[p, some] = (result * (a / (a + b))).astype(BF16)
                results.append(result)
                logs = jnp.where(log_lane == place + (s * 32 + p * 2 * HL), log, logs)
            for half in range(0 if is_early(s) else 2):
                rows = slice(half * 8, half * 8 + 8)
                r_send[s, some, half] = jnp.concatenate(
                    [results[0][:, rows], results[1][:, rows]], axis=1
                ).astype(BF16)
            row = jnp.sum(logs, axis=1, keepdims=True)
            if 0 < s < LAST:
                row = row + l_send[0, some]
            l_send[s // LAST, some] = row
            return carry

        lax.fori_loop(0, NW // PART, part, 0)
        if s >= LAST - 1:
            l_recv[s // LAST, 0] = l_send[s // LAST, 0]
            send_logs(s // LAST)
        if is_early(s):
            for p in range(2):
                moved = dot(order_in[...], raw[p].reshape(ROWS, HD)).astype(BF16)
                for h in range(HL):
                    slot_attn[p, :, h * HD:(h + 1) * HD] = moved[h * REQ:(h + 1) * REQ]
            return
        r_recv[s, 0] = r_send[s, 0]
        send_results(s)

    def merge(s):
        g = s // LAST
        if s in (FIRST, LAST):
            await_all(l_recv.at[g, pl.ds(1, NW - 1)], lr.at[g])
        logs = jnp.zeros((REQ, HD), F32)
        for o in range(NW):
            logs = jnp.where(own == o, l_recv[g, o], logs)
        for h in range(HL):
            pre = jnp.sum(jnp.where(lanes == pick + (s * 32 + 2 * h), logs, 0.0), axis=1, keepdims=True)
            loc = loc_log[s, h]
            high = jnp.maximum(pre, loc)
            a, b = jnp.exp(pre - high), jnp.exp(loc - high)
            mine = loc_out[s, h] * (b / (a + b))
            if is_early(s):
                attn[s, :, h * HD:(h + 1) * HD] = mine.astype(BF16)
            else:
                pre_part[h] = a / (a + b)
                loc_out[s, h] = mine

    def take(s, half):
        back = dot(gather[...], r_recv[s, :, half].reshape(ROWS, HD))
        for n in range(4):
            h = half * 4 + n
            joint = pre_part[h] * back[n * REQ:(n + 1) * REQ] + loc_out[s, h]
            attn[s, :, h * HD:(h + 1) * HD] = joint.astype(BF16)

    def block(dy, core):
        return lax.rem(y + dy, NY) * 2 + core

    def term(s, dy, side):
        return dot(attn[s], w[block(dy, 1 - c if side else c)])

    def give(s, dy):
        given[s, dy] = term(s, dy, 1).astype(BF16)
        pltpu.make_async_remote_copy(
            src_ref=given.at[s, dy], dst_ref=c_recv.at[s, dy], send_sem=cs.at[s, dy],
            recv_sem=cr.at[s, dy], device_id=other, device_id_type=MESH,
        ).start()

    def keep(s, dy):
        kept[s, dy] = term(s, dy, 0)

    def pair(s, dy):
        await_all(c_recv.at[s, dy], cr.at[s, dy])
        both = kept[s, dy] + c_recv[s, dy].astype(F32)
        if dy == 0:
            kept[s, dy] = both
            pltpu.make_async_copy(kept.at[s, dy], own_hbm.at[s], out_sems.at[s]).start()
            return
        y_send[s, dy - 1] = both.astype(BF16)
        pltpu.make_async_remote_copy(
            src_ref=y_send.at[s, dy - 1], dst_ref=y_recv.at[dy - 1, s],
            send_sem=ys.at[s], recv_sem=yr.at[s], device_id=across(dy), device_id_type=MESH,
        ).start()

    def project(s):
        give(s, 2)
        give(s, 1)
        give(s, 3)
        keep(s, 2)
        keep(s, 1)
        pair(s, 2)
        keep(s, 3)
        pair(s, 1)
        give(s, 0)
        pair(s, 3)
        keep(s, 0)
        pair(s, 0)

    def rows_of(u):
        if u < EARLY:
            return slot_attn[...].reshape(2 * REQ, HL * HD)
        return attn[FIRST:FIRST + EARLY].reshape(2 * REQ, HL * HD)

    def give_early(u, dy):
        term = dot(rows_of(u), w[block(dy, 1 - c)]).astype(BF16)
        given_e[u, dy] = term.reshape(2, REQ, SHARE)
        pltpu.make_async_remote_copy(
            src_ref=given_e.at[u, dy], dst_ref=c_recv_e.at[u, dy], send_sem=cse.at[u, dy],
            recv_sem=cre.at[u, dy], device_id=other, device_id_type=MESH,
        ).start()

    def keep_early(u, dy):
        kept_e[u, dy] = dot(rows_of(u), w[block(dy, c)]).reshape(2, REQ, SHARE)

    def pair_early(u, dy):
        await_all(c_recv_e.at[u, dy], cre.at[u, dy])
        both = kept_e[u, dy] + c_recv_e[u, dy].astype(F32)
        if dy == 0:
            kept_e[u, dy] = both
            return
        y_send_e[u, dy - 1] = both.astype(BF16)
        target = y_recv_e.at[u, dy - 1] if u < EARLY else y_recv.at[dy - 1, pl.ds(FIRST, EARLY)]
        pltpu.make_async_remote_copy(
            src_ref=y_send_e.at[u, dy - 1], dst_ref=target, send_sem=yse.at[u],
            recv_sem=yre.at[u], device_id=across(dy), device_id_type=MESH,
        ).start()

    def project_early(u):
        give_early(u, 2)
        give_early(u, 1)
        give_early(u, 3)
        keep_early(u, 2)
        keep_early(u, 1)
        pair_early(u, 2)
        keep_early(u, 3)
        pair_early(u, 1)
        give_early(u, 0)
        pair_early(u, 3)
        keep_early(u, 0)
        pair_early(u, 0)

    def return_early(s):
        await_all(y_recv_e.at[s], yre.at[s])
        total = kept_e[s, 0]
        for dy in range(NY - 1):
            total = total + y_recv_e[s, dy].astype(F32)
        total = total.astype(BF16).reshape(2 * REQ, SHARE)
        stacked = jnp.concatenate([total[:, j * HD:(j + 1) * HD] for j in range(4)], axis=0)
        placed = dot(order_out[...], stacked).astype(BF16).reshape(NW, 16, HD)
        p_send[s] = placed
        p_recv[s, 0] = placed[0]
        send_projected(s)

    def combine_early(s):
        await_all(p_recv.at[s, pl.ds(1, NW - 1)], pr.at[s])
        back = dot(pick_out[...], p_recv[s].reshape(ROWS, HD))
        for j in range(4):
            cols = slice(j * HD, (j + 1) * HD)
            own_v[s, :, cols] = kept_e[EARLY, 0, s, :, cols] + back[j * REQ:(j + 1) * REQ]
        pltpu.make_async_copy(own_v.at[s], own_hbm.at[FIRST + s], out_sems.at[FIRST + s]).start()

    def step(s):
        merge(s)
        await_all(r_recv.at[s, pl.ds(1, NW - 1)], rr.at[s])
        take(s, 0)
        take(s, 1)
        project(s)

    attend(0)
    await_all(f_recv.at[pl.ds(1, NW - 1)], fr)
    attend(1)
    for load in loads[10:]:
        load.wait()
    project_early(0)
    attend(2)
    project_early(1)
    return_early(0)
    attend(3)
    merge(1)
    merge(2)
    project_early(2)
    step(0)
    return_early(1)
    combine_early(0)
    step(3)
    combine_early(1)

    await_all(f_send.at[pl.ds(1, NW - 1)], fs)
    for u in range(EARLY + 1):
        for dy in range(NY):
            await_all(given_e.at[u, dy], cse.at[u, dy])
        await_all(y_send_e.at[u], yse.at[u])
    await_all(y_recv.at[:, pl.ds(FIRST, EARLY)], yre.at[EARLY])
    for g in range(2):
        await_all(l_send.at[g, pl.ds(1, NW - 1)], ls.at[g])
    for s in range(EARLY):
        await_all(p_send.at[s, pl.ds(1, NW - 1)], ps.at[s])
        pltpu.make_async_copy(own_v.at[s], own_hbm.at[FIRST + s], out_sems.at[FIRST + s]).wait()
    for s in range(STEPS):
        await_all(q_send.at[s, pl.ds(1, NW - 1)], qs.at[s])
        if is_early(s):
            continue
        await_all(r_send.at[s, pl.ds(1, NW - 1)], rs.at[s])
        for dy in range(NY):
            await_all(given.at[s, dy], cs.at[s, dy])
        await_all(y_send.at[s], ys.at[s])
        pltpu.make_async_copy(kept.at[s, 0], own_hbm.at[s], out_sems.at[s]).wait()
    for s in range(STEPS):
        if not is_early(s):
            await_all(y_recv.at[:, s], yr.at[s])


def body(
    queries, new_keys, new_values, suffix_keys, suffix_values, suffix_len,
    prefix_keys, prefix_values, prefix_of, out_weight,
):
    anywhere = pl.BlockSpec(memory_space=pl.ANY)
    fixed = functools.partial(pltpu.with_memory_space_constraint, memory_space=pltpu.HBM)
    dma = pltpu.SemaphoreType.DMA
    slots = (STEPS, NW, 2, 16, HD)
    logs = (2, NW, 1, HD)
    own, parts = pl.pallas_call(
        kernel,
        out_shape=(
            jax.ShapeDtypeStruct((STEPS, REQ, SHARE), F32),
            jax.ShapeDtypeStruct((NY - 1, STEPS, REQ, SHARE), BF16),
        ),
        in_specs=[anywhere] * 10,
        out_specs=(anywhere, anywhere),
        scratch_shapes=[
            pltpu.VMEM(queries.shape, BF16),
            pltpu.VMEM(new_keys.shape, BF16),
            pltpu.VMEM(new_values.shape, BF16),
            pltpu.VMEM(suffix_keys.shape, BF16),
            pltpu.VMEM(suffix_values.shape, BF16),
            pltpu.VMEM(prefix_keys.shape, BF16),
            pltpu.VMEM(prefix_values.shape, BF16),
            pltpu.VMEM((2 * NY, out_weight.shape[0], SHARE), BF16),
            pltpu.VMEM((2, PRE, 2 * HD), BF16),
            pltpu.VMEM(queries.shape, F32),
            pltpu.VMEM(new_keys.shape, F32),
            pltpu.VMEM(new_values.shape, F32),
            pltpu.VMEM((LKEYS + HD, HD), BF16),
            pltpu.VMEM((LKEYS + HD, 2 * HD), BF16),
            pltpu.VMEM((1, REQ), I32),
            pltpu.VMEM((1, REQ), I32),
            pltpu.VMEM((REQ, HD), I32),
            pltpu.VMEM((ROWS, HALF), BF16),
            pltpu.VMEM((HALF, ROWS), BF16),
            pltpu.VMEM(slots, BF16),
            pltpu.VMEM(slots, BF16),
            pltpu.VMEM(slots, BF16),
            pltpu.VMEM(slots, BF16),
            pltpu.VMEM(logs, F32),
            pltpu.VMEM(logs, F32),
            pltpu.VMEM((STEPS, HL, REQ, HD), F32),
            pltpu.VMEM((STEPS, HL, REQ, HD), F32),
            pltpu.VMEM((HL, REQ, HD), F32),
            pltpu.VMEM((STEPS, REQ, HL * HD), BF16),
            pltpu.VMEM((STEPS, NY, REQ, SHARE), F32),
            pltpu.VMEM((STEPS, NY, REQ, SHARE), BF16),
            pltpu.VMEM((STEPS, NY, REQ, SHARE), BF16),
            pltpu.VMEM((STEPS, NY - 1, REQ, SHARE), BF16),
            pltpu.VMEM((ROWS, ROWS), BF16),
            pltpu.VMEM((ROWS, ROWS), BF16),
            pltpu.VMEM((HALF, ROWS), BF16),
            pltpu.VMEM((NW, 1, HD), F32),
            pltpu.VMEM((NW, 1, HD), F32),
            pltpu.VMEM((2, NW, 16, HD), BF16),
            pltpu.VMEM((2, REQ, HL * HD), BF16),
            pltpu.VMEM((EARLY + 1, NY, 2, REQ, SHARE), F32),
            pltpu.VMEM((EARLY + 1, NY, 2, REQ, SHARE), BF16),
            pltpu.VMEM((EARLY + 1, NY, 2, REQ, SHARE), BF16),
            pltpu.VMEM((EARLY + 1, NY - 1, 2, REQ, SHARE), BF16),
            pltpu.VMEM((EARLY, NY - 1, 2, REQ, SHARE), BF16),
            pltpu.VMEM((EARLY, NW, 16, HD), BF16),
            pltpu.VMEM((EARLY, NW, 16, HD), BF16),
            pltpu.VMEM((EARLY, REQ, SHARE), F32),
            dma((STEPS + 8 + 2 * NY,)),
            dma((STEPS,)),
        ] + [dma((STEPS,))] * 6 + [dma((STEPS, NY))] * 2 + [dma((STEPS,))] * 2
        + [dma, dma] + [dma((EARLY + 1, NY))] * 2 + [dma((EARLY + 1,))] * 2 + [dma((EARLY,))] * 2,
        compiler_params=pltpu.CompilerParams(
            collective_id=0, has_side_effects=True, vmem_limit_bytes=48 * 2**20
        ),
        name="attention",
    )(
        fixed(queries), fixed(prefix_of.reshape(1, REQ)), fixed(suffix_len.reshape(1, REQ)),
        *(
            fixed(a)
            for a in (new_keys, new_values, suffix_keys, suffix_values,
                      prefix_keys, prefix_values, out_weight)
        ),
    )
    for dy in range(NY - 1):
        own = own + parts[dy].astype(F32)
    return own.astype(BF16)


def solution(mesh):
    return jax.shard_map(
        body,
        mesh=mesh,
        in_specs=(
            P(None, "wide", "tensor"),
            P(None, "wide", "tensor"),
            P(None, "wide", "tensor"),
            P("wide", None, "tensor"),
            P("wide", None, "tensor"),
            P("wide"),
            P("wide", None, "tensor"),
            P("wide", None, "tensor"),
            P("wide", None),
            P("tensor", None),
        ),
        out_specs=P(None, "wide", "tensor"),
        check_vma=False,
    )
```
